128 devices in a mesh: band: 2 (over x_lo), dom: 64 (over x_hi, y, z, core).
Axes of the slice: x: 4 (x_hi: 2, x_lo: 2; x = x_hi * 2 + x_lo), y: 4, z: 4, core: 2. Of those that a mesh axis runs over, the one named last changes fastest.
Arguments:
- orbitals: float32 [48, 64, 12, 2304], P('band', 'dom'), as said below
- potential: float32 [64, 12, 2304], P('dom'), may hold values from -1.5 to 1.5
Outputs:
- rotated: float32 [48, 64, 12, 2304], P('band', 'dom')
The draws below stay inside these ranges and needn't reach their ends.
Inputs may be any that keep to these rules, and one draw needn't show every extreme that they name: `orbitals`: orbitals are linearly independent.
All inputs are finite; a program needn't handle non-finite values.
Results may differ from the reference program's by a relative error of at most 0.00023.
Values sent between devices are 32-bit elements; how exact they have to be, the bound alone decides.
A program may use at most 128 MiB of HBM per device.

```python
import jax
import jax.numpy as jnp
import numpy as np
from jax import lax

NORB = 48
CX = 12
CY = 48
CZ = 48
CYZ = 2304
BRICKS = 64


def draw_orbitals(key, part):
    key = jax.random.fold_in(key, 11)
    noise_key = jax.random.fold_in(key, 0)
    base = jax.random.normal(noise_key, (NORB, BRICKS, CX, CYZ), jnp.float32)
    return base + 0.45 * jnp.roll(base, -1, 0) + 0.3 * jnp.roll(base, -5, 0)


def steps_of(rng, shape, pieces, smallest, high):
    loudness, own = 1.0, jax.random.fold_in(rng, 6)
    for dim, blocks in pieces:
        steps = jnp.exp(jax.random.uniform(jax.random.fold_in(own, dim), (blocks,), jnp.float32, smallest / len(pieces), high / len(pieces)))
        loudness = loudness * jnp.repeat(steps, shape[dim] // blocks).reshape([-1 if axis == dim else 1 for axis in range(len(shape))])
    return loudness


def setup_inputs(seed: int = 0) -> dict:
    seeds = jax.random.split(jax.random.key(seed), 3)
    orbitals = draw_orbitals(jax.random.fold_in(seeds[2], 71), 0)
    potential = jnp.clip(jax.random.uniform(seeds[1], (BRICKS, CX, CYZ), jnp.float32, -1.5, 1.5) * steps_of(seeds[1], (BRICKS, CX, CYZ), ((0, 64),), -0.4, 0.0), -1.5, 1.5)
    return dict(orbitals=orbitals, potential=potential)


stencil_weights = (-5369.0 / 1800.0, 12.0 / 7.0, -15.0 / 56.0, 10.0 / 189.0, -1.0 / 112.0, 2.0 / 1925.0, -1.0 / 16632.0)
centre_shift = 7.25
half_width = 5.25
code_order = np.array([0, 1, 3, 2], dtype=np.int32)

def bricks_to_grid(blocks):
    leading = blocks.shape[0]
    zcount = blocks.shape[1] // 16
    split = blocks.reshape(leading, zcount, 4, 4, CX, CY, CZ)
    split = jnp.take(split, code_order[:zcount], axis=1)
    split = jnp.take(split, code_order, axis=2)
    split = jnp.take(split, code_order, axis=3)
    return split.transpose(0, 3, 4, 2, 5, 1, 6).reshape(leading, 4 * CX, 4 * CY, zcount * CZ)

def grid_to_bricks(grid):
    leading = grid.shape[0]
    zcount = grid.shape[3] // CZ
    split = grid.reshape(leading, 4, CX, 4, CY, zcount, CZ).transpose(0, 5, 3, 1, 2, 4, 6)
    split = jnp.take(split, code_order[:zcount], axis=1)
    split = jnp.take(split, code_order, axis=2)
    split = jnp.take(split, code_order, axis=3)
    return split.reshape(leading, 16 * zcount, CX, CY * CZ)

def apply_h(field, pot):
    laplace = 3.0 * stencil_weights[0] * field
    for shift in range(1, 7):
        near = jnp.roll(field, shift, 0) + jnp.roll(field, -shift, 0)
        near = near + jnp.roll(field, shift, 1) + jnp.roll(field, -shift, 1)
        near = near + jnp.roll(field, shift, 2) + jnp.roll(field, -shift, 2)
        laplace = laplace + stencil_weights[shift] * near
    return -0.5 * laplace + pot * field

def filter_one(field, pot):
    first = (apply_h(field, pot) - centre_shift * field) / half_width
    return 2.0 * (apply_h(first, pot) - centre_shift * first) / half_width - field

def reference(orbitals, potential):
    grid = bricks_to_grid(orbitals)
    pot = bricks_to_grid(potential[None])[0]
    filtered = lax.map(lambda one: filter_one(one, pot), grid)
    flat = filtered.reshape(NORB, -1)
    gram = jnp.dot(flat, flat.T, precision=lax.Precision.HIGHEST)
    gram = gram * (1.0 / flat.shape[1])
    lower = jnp.linalg.cholesky(gram)
    inverse = lax.linalg.triangular_solve(lower, jnp.eye(NORB, dtype=gram.dtype), left_side=True, lower=True)
    rotated = jnp.dot(inverse, flat, precision=lax.Precision.HIGHEST)
    return grid_to_bricks(rotated.reshape(grid.shape))
```

```python
import functools

import jax
import jax.numpy as jnp
import numpy as np
from jax import lax
from jax.experimental import pallas as pl
from jax.experimental.pallas import tpu as pltpu
from jax.sharding import PartitionSpec as P

CX = 12
CY = 48
CZ = 48
CYZ = CY * CZ
LANES = 3 * 128 + CYZ + 3 * 128
MESH = pl.DeviceIdType.MESH
BF = jnp.bfloat16
F32 = jnp.float32

stencil_weights = (
    -5369.0 / 1800.0,
    12.0 / 7.0,
    -15.0 / 56.0,
    10.0 / 189.0,
    -1.0 / 112.0,
    2.0 / 1925.0,
    -1.0 / 16632.0,
)
centre_shift = 7.25
half_width = 5.25
near = [-0.5 * w / half_width for w in stencil_weights]
own = (-1.5 * stencil_weights[0] - centre_shift) / half_width


def split_np(a):
    a = a.astype(np.float32)
    high = a.astype(BF)
    return high, (a - high.astype(np.float32)).astype(BF)


def yz_weights():
    out = np.zeros((3, 1280, 256), np.float64)
    for part in range(3):
        for n in range(256):
            cell = 256 * part + n
            row, z = cell // CZ, cell % CZ
            for k in range(1, 7):
                for sign in (-1, 1):
                    out[part, n + 384 + sign * CZ * k, n] += near[k]
                    at = z + sign * k
                    if 0 <= at < CZ:
                        out[part, n + 384 + sign * k, n] += near[k]
                    elif at < 0:
                        out[part, 1024 + row * 6 + at + 6, n] += near[k]
                    else:
                        out[part, 1152 + row * 6 + at - CZ, n] += near[k]
    return split_np(out)


def face_weights():
    out = np.zeros((768, 256), np.float32)
    for row in range(16):
        for i in range(6):
            out[row * CZ + i, row * 6 + i] = 1
            out[row * CZ + CZ - 6 + i, 128 + row * 6 + i] = 1
    return out.astype(BF)


def split(v):
    high = v.astype(BF)
    return high, (v - high.astype(F32)).astype(BF)


def dot(a, b):
    return jnp.dot(a, b, preferred_element_type=F32)


def dot_t(a, b):
    return lax.dot_general(a, b, (((1,), (1,)), ((), ())), preferred_element_type=F32)


def flipped(index, bit):
    return index + bit * (1 - 2 * (index // bit % 2))


def filter_kernel(
    orb, pot_hbm, wh_hbm, wl_hbm, sel_hbm, f_hbm, fo_hbm, gram,
    lin, pot, wh, wl, sel, cen, xlo, xhi, zlo, zhi, zlo_out, zhi_out, vh, vl, zh, zl, yz, fil, oth, part, got,
    in_sem, out_sem, send_sem, recv_sem, band_send, band_recv, sum_send, sum_recv,
):
    band, dom = lax.axis_index("band"), lax.axis_index("dom")
    loads = [
        pltpu.make_async_copy(a, b, in_sem.at[i])
        for i, (a, b) in enumerate(((orb, lin), (pot_hbm, pot), (wh_hbm, wh), (wl_hbm, wl), (sel_hbm, sel)))
    ]
    for load in loads:
        load.start()

    partners = [(band, flipped(dom, 1 << bit)) for bit in range(6)] + [(1 - band, dom)]
    barrier = pltpu.get_barrier_semaphore()
    for partner in partners:
        pl.semaphore_signal(barrier, 1, device_id=partner, device_id_type=MESH)

    ends = []
    for first in (1, 4, 16):
        odd = (dom // first % 4 + 1) // 2 % 2
        below = odd * flipped(dom, first) + (1 - odd) * flipped(dom, 2 * first)
        above = odd * flipped(dom, 2 * first) + (1 - odd) * flipped(dom, first)
        ends.append(((band, below), (band, above)))

    def copies(slot):
        middle = pl.ds(384, CYZ)
        table = (
            (cen.at[slot, pl.ds(0, 6), :, middle], xhi.at[slot], ends[0][0]),
            (cen.at[slot, pl.ds(6, 6), :, middle], xlo.at[slot], ends[0][1]),
            (cen.at[slot, :, :, pl.ds(384, 384)], cen.at[slot, :, :, pl.ds(384 + CYZ, 384)], ends[1][0]),
            (cen.at[slot, :, :, pl.ds(CYZ, 384)], cen.at[slot, :, :, pl.ds(0, 384)], ends[1][1]),
            (zlo_out.at[slot], zhi.at[slot], ends[2][0]),
            (zhi_out.at[slot], zlo.at[slot], ends[2][1]),
        )
        return [
            pltpu.make_async_remote_copy(a, b, send_sem.at[slot, i], recv_sem.at[slot, i], device_id=to, device_id_type=MESH)
            for i, (a, b, to) in enumerate(table)
        ]

    def band_copy(chunk, half):
        layers = pl.ds(6 * half, 6)
        return pltpu.make_async_remote_copy(
            fil.at[chunk, layers], oth.at[chunk, layers], band_send.at[chunk, half], band_recv.at[chunk, half],
            device_id=(1 - band, dom), device_id_type=MESH,
        )

    def prepare(slot):
        @pl.loop(0, 6)
        def _(i):
            v = cen[slot, pl.ds(2 * i, 2), :, pl.ds(384, CYZ)].reshape(16, CYZ)
            high, low = split(v)
            vh[slot, pl.ds(16 * i, 16), pl.ds(384, CYZ)] = high
            vl[slot, pl.ds(16 * i, 16), pl.ds(384, CYZ)] = low

        for m in range(3):
            lanes = pl.ds(384 + 768 * m, 768)
            faces = dot(vh[slot, :, lanes], sel[...]) + dot(vl[slot, :, lanes], sel[...])
            zlo_out[slot, :, :, pl.ds(128 * m, 128)] = faces[:, :128].reshape(CX, 8, 128)
            zhi_out[slot, :, :, pl.ds(128 * m, 128)] = faces[:, 128:].reshape(CX, 8, 128)
        for copy in copies(slot):
            copy.start()

    def split_rims(slot):
        for start in (0, 384 + CYZ):
            v = cen[slot, :, :, pl.ds(start, 384)].reshape(96, 384)
            high, low = split(v)
            vh[slot, :, pl.ds(start, 384)] = high
            vl[slot, :, pl.ds(start, 384)] = low
        for m in range(3):
            for rim, at in ((zlo, 0), (zhi, 128)):
                v = rim[slot, :, :, pl.ds(128 * m, 128)].reshape(96, 128)
                high, low = split(v)
                zh[:, pl.ds(256 * m + at, 128)] = high
                zl[:, pl.ds(256 * m + at, 128)] = low

    def yz_product(slot):
        @pl.loop(0, 3)
        def _(j):
            start = pl.multiple_of(256 * j, 256)

            def window(v, z):
                return jnp.concatenate(
                    [
                        jnp.concatenate([v[slot, :, pl.ds(start + 768 * m, 1024)], z[:, pl.ds(256 * m, 256)]], 1)
                        for m in range(3)
                    ],
                    0,
                )

            high, low = window(vh, zh), window(vl, zl)
            total = dot(high, wh[j]) + dot(low, wh[j]) + dot(high, wl[j])
            for m in range(3):
                yz[:, pl.ds(start + 768 * m, 256)] = total[96 * m : 96 * m + 96]

    def stencil(slot, write):
        @pl.loop(0, CYZ // 128)
        def _(t):
            at = pl.multiple_of(128 * t, 128)
            here, mid = pl.ds(at, 128), pl.ds(at + 384, 128)
            v = [xlo[slot, i, :, here] for i in range(6)]
            v += [cen[slot, i, :, mid] for i in range(CX)]
            v += [xhi[slot, i, :, here] for i in range(6)]
            for x in range(CX):
                diagonal = pot[pl.ds(18 * x + t, 1), :] * (1.0 / half_width) + own
                total = diagonal * v[x + 6] + yz[pl.ds(8 * x, 8), here]
                for k in range(1, 7):
                    total = total + near[k] * (v[x + 6 - k] + v[x + 6 + k])
                write(x, here, mid, total)

    loads[0].wait()

    def relayout(chunk):
        @pl.loop(0, CX)
        def _(x):
            for t in range(18):
                cen[chunk, x, :, pl.ds(384 + 128 * t, 128)] = lin[pl.ds(8 * 216 * chunk + 18 * x + t, 8, stride=216), :]

    relayout(0)
    loads[4].wait()
    pl.semaphore_wait(barrier, len(partners))

    @pl.loop(0, 3)
    def _(chunk):
        @pl.when(chunk > 0)
        def _():
            relayout(chunk)

        @pl.when(chunk < 2)
        def _():
            prepare(chunk)

    loads[1].wait()
    loads[2].wait()
    loads[3].wait()

    @pl.loop(0, 6)
    def _(step):
        slot = jnp.where(step == 2, 3, jnp.where(step == 3, 2, step))
        for copy in copies(slot):
            copy.wait_recv()
        split_rims(slot)
        yz_product(slot)

        @pl.when(slot < 3)
        def _():
            def write(x, here, mid, total):
                cen[slot + 3, x, :, mid] = total

            stencil(slot, write)
            prepare(slot + 3)

            @pl.when(slot == 0)
            def _():
                prepare(2)

        @pl.when(slot >= 3)
        def _():
            def write(x, here, mid, total):
                fil[slot - 3, x, :, here] = 2.0 * total - cen[slot - 3, x, :, mid]

            stencil(slot, write)
            band_copy(slot - 3, 1 - band).start()
            band_copy(slot - 3, band).start()
            pltpu.make_async_copy(fil.at[slot - 3], f_hbm.at[slot - 3], out_sem.at[slot - 3]).start()

    def rows(ref, x):
        v = ref[:, x].reshape(24, CYZ)
        high, low = split(v)
        return jnp.concatenate([high, low], 0)

    def folded(products):
        return products[:24, :24] + products[24:, :24] + products[:24, 24:]

    part[...] = jnp.zeros_like(part)

    @pl.loop(0, CX)
    def _(x):
        a = rows(fil, x)
        part[0, :, 0:24] += folded(dot_t(a, a))

    for chunk in range(3):
        band_copy(chunk, band).wait_recv()

    @pl.loop(0, 6)
    def _(i):
        x = 6 * band + i
        part[0, :, 24:48] += folded(dot_t(rows(fil, x), rows(oth, x)))

    for bit in range(7):
        copy = pltpu.make_async_remote_copy(
            part.at[bit], got.at[bit], sum_send.at[bit], sum_recv.at[bit], device_id=partners[bit], device_id_type=MESH
        )
        copy.start()
        copy.wait()
        if bit < 6:
            part[bit + 1] = part[bit] + got[bit]

    gram[0] = part[6]
    gram[1] = got[6]
    for chunk in range(3):
        band_copy(chunk, 1 - band).wait_recv()
        pltpu.make_async_copy(oth.at[chunk], fo_hbm.at[chunk], out_sem.at[3 + chunk]).start()
    for chunk in range(3):
        for half in range(2):
            band_copy(chunk, half).wait_send()
        pltpu.make_async_copy(fil.at[chunk], f_hbm.at[chunk], out_sem.at[chunk]).wait()
        pltpu.make_async_copy(oth.at[chunk], fo_hbm.at[chunk], out_sem.at[3 + chunk]).wait()

    @pl.loop(0, 6)
    def _(slot):
        for copy in copies(slot):
            copy.wait_send()


def filter_call(lines, pot):
    wh, wl = yz_weights()
    sel = face_weights()
    any_space = pl.BlockSpec(memory_space=pl.ANY)
    chunk = (3, CX, 8, CYZ)
    vm = pltpu.VMEM
    return pl.pallas_call(
        filter_kernel,
        out_shape=(
            jax.ShapeDtypeStruct(chunk, F32),
            jax.ShapeDtypeStruct(chunk, F32),
            jax.ShapeDtypeStruct((2, 24, 128), F32),
        ),
        in_specs=[any_space] * 5,
        out_specs=(any_space, any_space, pl.BlockSpec(memory_space=pltpu.VMEM)),
        scratch_shapes=[
            vm((24 * 216, 128), F32),
            vm((216, 128), F32),
            vm(wh.shape, BF),
            vm(wl.shape, BF),
            vm(sel.shape, BF),
            vm((6, CX, 8, LANES), F32),
            vm((6, 6, 8, CYZ), F32),
            vm((6, 6, 8, CYZ), F32),
            vm((6, CX, 8, 384), F32),
            vm((6, CX, 8, 384), F32),
            vm((6, CX, 8, 384), F32),
            vm((6, CX, 8, 384), F32),
            vm((6, 96, LANES), BF),
            vm((6, 96, LANES), BF),
            vm((96, 768), BF),
            vm((96, 768), BF),
            vm((96, CYZ), F32),
            vm(chunk, F32),
            vm(chunk, F32),
            vm((7, 24, 128), F32),
            vm((7, 24, 128), F32),
            pltpu.SemaphoreType.DMA((5,)),
            pltpu.SemaphoreType.DMA((6,)),
            pltpu.SemaphoreType.DMA((6, 6)),
            pltpu.SemaphoreType.DMA((6, 6)),
            pltpu.SemaphoreType.DMA((3, 2)),
            pltpu.SemaphoreType.DMA((3, 2)),
            pltpu.SemaphoreType.DMA((7,)),
            pltpu.SemaphoreType.DMA((7,)),
        ],
        compiler_params=pltpu.CompilerParams(collective_id=0, has_side_effects=True, vmem_limit_bytes=56 << 20),
        name="filter",
    )(lines, pot, jnp.asarray(wh), jnp.asarray(wl), jnp.asarray(sel))


def rotate_kernel(low, high, mat, out, mine, theirs, lines, sems, out_sem):
    loads = []
    for x in range(CX):
        loads.append(
            (
                pltpu.make_async_copy(low.at[:, x], mine.at[:, x], sems.at[0, x]),
                pltpu.make_async_copy(high.at[:, x], theirs.at[:, x], sems.at[1, x]),
            )
        )
        for load in loads[-1]:
            load.start()
    mh, ml = split(mat[...])
    left = jnp.concatenate([mh, ml, mh], 1)
    for x in range(CX):
        for load in loads[x]:
            load.wait()
        v = jnp.concatenate([mine[:, x].reshape(24, CYZ), theirs[:, x].reshape(24, CYZ)], 0)
        vh, vl = split(v)
        made = dot(left, jnp.concatenate([vh, vh, vl], 0))
        for t in range(18):
            lines[pl.ds(18 * x + t, 24, stride=216), :] = made[:, 128 * t : 128 * t + 128]
    copy = pltpu.make_async_copy(lines, out, out_sem)
    copy.start()
    copy.wait()


def rotate_call(mine, theirs, mat):
    any_space = pl.BlockSpec(memory_space=pl.ANY)
    vm = pltpu.VMEM
    return pl.pallas_call(
        rotate_kernel,
        out_shape=jax.ShapeDtypeStruct((24 * 216, 128), F32),
        in_specs=[any_space, any_space, pl.BlockSpec(memory_space=pltpu.VMEM)],
        out_specs=any_space,
        scratch_shapes=[
            vm((3, CX, 8, CYZ), F32),
            vm((3, CX, 8, CYZ), F32),
            vm((24 * 216, 128), F32),
            pltpu.SemaphoreType.DMA((2, CX)),
            pltpu.SemaphoreType.DMA,
        ],
        compiler_params=pltpu.CompilerParams(vmem_limit_bytes=56 << 20),
        name="rotate",
    )(mine, theirs, mat)


def body(orbitals, potential):
    group = orbitals.shape[0]
    band = lax.axis_index("band")
    scale = 1.0 / (CX * CYZ * lax.axis_size("dom"))
    mine, theirs, gram = filter_call(orbitals.reshape(group * 216, 128), potential.reshape(216, 128))
    low, high = jnp.where(band == 0, gram, gram[::-1]) * scale
    cross = low[:, 24:48].T + high[:, 24:48]
    whole = jnp.block([[low[:, :24], cross.T], [cross, high[:, :24]]])
    lower = jnp.linalg.cholesky(whole)
    inverse = lax.linalg.triangular_solve(lower, jnp.eye(2 * group, dtype=F32), left_side=True, lower=True)
    rows = lax.dynamic_slice_in_dim(inverse, band * group, group, 0)
    rows = jnp.where(band == 0, rows, jnp.roll(rows, group, 1))
    return rotate_call(mine, theirs, rows).reshape(orbitals.shape)


def solution(mesh):
    return jax.shard_map(
        body,
        mesh=mesh,
        in_specs=(P("band", "dom", None, None), P("dom", None, None)),
        out_specs=P("band", "dom", None, None),
        check_vma=False,
    )
```

```python
import jax
import jax.numpy as jnp
import numpy as np
from jax import lax
from jax.experimental import pallas as pl
from jax.experimental.pallas import tpu as pltpu
from jax.sharding import PartitionSpec as P

CX = 12
CY = 48
CZ = 48
CYZ = CY * CZ
LANES = 3 * 128 + CYZ + 3 * 128
MESH = pl.DeviceIdType.MESH
BF = jnp.bfloat16
F32 = jnp.float32

stencil_weights = (
    -5369.0 / 1800.0,
    12.0 / 7.0,
    -15.0 / 56.0,
    10.0 / 189.0,
    -1.0 / 112.0,
    2.0 / 1925.0,
    -1.0 / 16632.0,
)
centre_shift = 7.25
half_width = 5.25
near = [-0.5 * w / half_width for w in stencil_weights]
own = (-1.5 * stencil_weights[0] - centre_shift) / half_width


def split_np(a):
    a = a.astype(np.float32)
    high = a.astype(BF)
    return high, (a - high.astype(np.float32)).astype(BF)


def yz_weights():
    out = np.zeros((3, 1280, 256), np.float64)
    for part in range(3):
        for n in range(256):
            cell = 256 * part + n
            row, z = cell // CZ, cell % CZ
            for k in range(1, 7):
                for sign in (-1, 1):
                    out[part, n + 384 + sign * CZ * k, n] += near[k]
                    at = z + sign * k
                    if 0 <= at < CZ:
                        out[part, n + 384 + sign * k, n] += near[k]
                    elif at < 0:
                        out[part, 1024 + row * 6 + at + 6, n] += near[k]
                    else:
                        out[part, 1152 + row * 6 + at - CZ, n] += near[k]
    return split_np(out)


def face_weights():
    out = np.zeros((768, 256), np.float32)
    for row in range(16):
        for i in range(6):
            out[row * CZ + i, row * 6 + i] = 1
            out[row * CZ + CZ - 6 + i, 128 + row * 6 + i] = 1
    return out.astype(BF)


def split(v):
    high = v.astype(BF)
    return high, (v - high.astype(F32)).astype(BF)


def dot(a, b):
    return jnp.dot(a, b, preferred_element_type=F32)


def dot_t(a, b):
    return lax.dot_general(a, b, (((1,), (1,)), ((), ())), preferred_element_type=F32)


def flipped(index, bit):
    return index + bit * (1 - 2 * (index // bit % 2))


def filter_kernel(
    orb, pot_hbm, wh_hbm, wl_hbm, sel_hbm, f_hbm, fo_hbm, gram,
    lin, pot, wh, wl, sel, cen, xlo, xhi, zlo, zhi, zlo_out, zhi_out, vh, vl, yz, fil, oth, part, got,
    in_sem, out_sem, send_sem, recv_sem, band_send, band_recv, sum_send, sum_recv,
):
    band, dom = lax.axis_index("band"), lax.axis_index("dom")
    loads = [
        pltpu.make_async_copy(a, b, in_sem.at[i])
        for i, (a, b) in enumerate(((orb, lin), (pot_hbm, pot), (wh_hbm, wh), (wl_hbm, wl), (sel_hbm, sel)))
    ]
    for load in loads:
        load.start()

    def across(z, core, y, x, other):
        to = dom
        for bit, used in enumerate((core, z % 2, z // 2, y % 2, y // 2, x)):
            if used:
                to = flipped(to, 1 << bit)
        return (1 - band if other else band), to

    stages = [
        [across(0, 0, 0, k % 2, k // 2) for k in range(1, 4)],
        [across(k // 2, k % 2, 0, 0, 0) for k in range(1, 8)],
        [across(0, 0, k, 0, 0) for k in range(1, 4)],
    ]
    partners = [partner for stage in stages for partner in stage]
    barrier = pltpu.get_barrier_semaphore()
    for partner in partners:
        pl.semaphore_signal(barrier, 1, device_id=partner, device_id_type=MESH)

    ends = []
    for first in (1, 4, 16):
        odd = (dom // first % 4 + 1) // 2 % 2
        below = odd * flipped(dom, first) + (1 - odd) * flipped(dom, 2 * first)
        above = odd * flipped(dom, 2 * first) + (1 - odd) * flipped(dom, first)
        ends.append(((band, below), (band, above)))

    def copies(slot, m):
        lanes, centre, face = pl.ds(768 * m, 768), pl.ds(384 + 768 * m, 768), pl.ds(128 * m, 128)
        table = (
            (cen.at[slot, pl.ds(0, 6), :, centre], xhi.at[slot, :, :, lanes], ends[0][0]),
            (cen.at[slot, pl.ds(6, 6), :, centre], xlo.at[slot, :, :, lanes], ends[0][1]),
            (zlo_out.at[slot, :, :, face], zhi.at[slot, :, :, face], ends[2][0]),
            (zhi_out.at[slot, :, :, face], zlo.at[slot, :, :, face], ends[2][1]),
        )
        return [
            pltpu.make_async_remote_copy(
                a, b, send_sem.at[slot, m, i], recv_sem.at[slot, m, i], device_id=to, device_id_type=MESH
            )
            for i, (a, b, to) in enumerate(table)
        ]

    def low_copy(slot):
        return pltpu.make_async_remote_copy(
            cen.at[slot, :, :, pl.ds(384, 384)], cen.at[slot, :, :, pl.ds(384 + CYZ, 384)],
            send_sem.at[slot, 0, 4], recv_sem.at[slot, 0, 4], device_id=ends[1][0], device_id_type=MESH,
        )

    def high_copy(slot):
        return pltpu.make_async_remote_copy(
            cen.at[slot, :, :, pl.ds(CYZ, 384)], cen.at[slot, :, :, pl.ds(0, 384)],
            send_sem.at[slot, 2, 4], recv_sem.at[slot, 2, 4], device_id=ends[1][1], device_id_type=MESH,
        )

    def band_copy(chunk, m, half):
        part_of = (chunk, pl.ds(6 * half, 6), slice(None), pl.ds(768 * m, 768))
        return pltpu.make_async_remote_copy(
            fil.at[part_of], oth.at[part_of], band_send.at[chunk, m, half], band_recv.at[chunk, m, half],
            device_id=(1 - band, dom), device_id_type=MESH,
        )

    def group(i):
        return 2 * i % 3

    def prepare(slot, m):
        lanes = pl.ds(pl.multiple_of(384 + 768 * m, 128), 768)
        face = pl.ds(pl.multiple_of(128 * m, 128), 128)
        high, low = split(cen[slot, :, :, lanes].reshape(96, 768))
        vh[slot, :, lanes] = high
        vl[slot, :, lanes] = low
        faces = dot(high, sel[...]) + dot(low, sel[...])
        zlo_out[slot, :, :, face] = faces[:, :128].reshape(CX, 8, 128)
        zhi_out[slot, :, :, face] = faces[:, 128:].reshape(CX, 8, 128)
        for copy in copies(slot, m):
            copy.start()

        @pl.when(m == 0)
        def _():
            low_copy(slot).start()

        @pl.when(m == 2)
        def _():
            high_copy(slot).start()

    def split_rim(slot, start):
        high, low = split(cen[slot, :, :, pl.ds(start, 384)].reshape(96, 384))
        vh[slot, :, pl.ds(start, 384)] = high
        vl[slot, :, pl.ds(start, 384)] = low

    def receive(slot, m):
        for copy in copies(slot, m):
            copy.wait_recv()

        @pl.when(m == 0)
        def _():
            high_copy(slot).wait_recv()
            split_rim(slot, 0)

        @pl.when(m == 2)
        def _():
            low_copy(slot).wait_recv()
            split_rim(slot, 384 + CYZ)

    def yz_product(slot, m):
        face = pl.ds(pl.multiple_of(128 * m, 128), 128)
        rims = jnp.concatenate([zlo[slot, :, :, face].reshape(96, 128), zhi[slot, :, :, face].reshape(96, 128)], 1)
        zh, zl = split(rims)
        for j in range(3):
            window = pl.ds(pl.multiple_of(256 * j + 768 * m, 256), 1024)
            high = jnp.concatenate([vh[slot, :, window], zh], 1)
            low = jnp.concatenate([vl[slot, :, window], zl], 1)
            yz[:, pl.ds(256 * j, 256)] = dot(high, wh[j]) + dot(low, wh[j]) + dot(high, wl[j])

    def stencil(slot, m, write):
        @pl.loop(0, 6)
        def _(t):
            at = pl.multiple_of(768 * m + 128 * t, 128)
            here, mid = pl.ds(at, 128), pl.ds(pl.multiple_of(at + 384, 128), 128)
            v = [xlo[slot, i, :, here] for i in range(6)]
            v += [cen[slot, i, :, mid] for i in range(CX)]
            v += [xhi[slot, i, :, here] for i in range(6)]
            for x in range(CX):
                diagonal = pot[pl.ds(18 * x + 6 * m + t, 1), :] * (1.0 / half_width) + own
                total = diagonal * v[x + 6] + yz[pl.ds(8 * x, 8), pl.ds(pl.multiple_of(128 * t, 128), 128)]
                for k in range(1, 7):
                    total = total + near[k] * (v[x + 6 - k] + v[x + 6 + k])
                write(x, here, mid, total)

    def relayout(chunk, m):
        for x in range(CX):
            for t in range(6):
                row = 8 * 216 * chunk + 18 * x + 6 * m + t
                lanes = pl.ds(pl.multiple_of(384 + 768 * m + 128 * t, 128), 128)
                cen[chunk, x, :, lanes] = lin[pl.ds(row, 8, stride=216), :]

    def enter(chunk, m):
        relayout(chunk, m)
        prepare(chunk, m)

    loads[0].wait()
    loads[4].wait()
    pl.semaphore_wait(barrier, len(partners))

    @pl.loop(0, 3)
    def _(i):
        enter(0, group(i))

    for load in loads[1:4]:
        load.wait()

    @pl.loop(0, 3)
    def _(chunk):
        @pl.loop(0, 3)
        def _(i):
            m = group(i)
            receive(chunk, m)

            def write(x, here, mid, total):
                cen[chunk + 3, x, :, mid] = total

            yz_product(chunk, m)
            stencil(chunk, m, write)
            prepare(chunk + 3, m)

        @pl.loop(0, 3)
        def _(i):
            m = group(i)
            receive(chunk + 3, m)

            @pl.when(chunk < 2)
            def _():
                enter(chunk + 1, m)

            def write(x, here, mid, total):
                fil[chunk, x, :, here] = 2.0 * total - cen[chunk, x, :, mid]

            yz_product(chunk + 3, m)
            stencil(chunk + 3, m, write)
            band_copy(chunk, m, 1 - band).start()

            @pl.when((band == 0) & (chunk < 2))
            def _():
                band_copy(chunk, m, 0).start()

        pltpu.make_async_copy(fil.at[chunk], f_hbm.at[chunk], out_sem.at[chunk]).start()

    def rows(ref, x):
        v = ref[:, x].reshape(24, CYZ)
        high, low = split(v)
        return jnp.concatenate([high, low], 0)

    def folded(a, b):
        products = dot_t(a, b)
        return products[:24, :24] + products[24:, :24] + products[:24, 24:]

    part[...] = jnp.zeros_like(part)

    @pl.loop(0, CX)
    def _(x):
        a = rows(fil, x)
        part[0, :, 0:24] += folded(a, a)

    part[0] = jnp.where(band == 0, part[0], pltpu.roll(part[0], 32, 1))

    @pl.loop(0, 3)
    def _(chunk):
        for m in range(3):
            band_copy(chunk, m, band).wait_recv()

    @pl.loop(0, 6)
    def _(i):
        mine, theirs = rows(fil, 6 * band + i), rows(oth, 6 * band + i)
        first, second = jnp.where(band == 0, mine, theirs), jnp.where(band == 0, theirs, mine)
        part[0, :, 64:88] += folded(second, first)
        part[0, :, 96:120] += folded(first, second)

    index = 0
    for number, stage in enumerate(stages):
        moves = []
        for partner in stage:
            moves.append(
                pltpu.make_async_remote_copy(
                    part.at[number], got.at[index], sum_send.at[index], sum_recv.at[index],
                    device_id=partner, device_id_type=MESH,
                )
            )
            moves[-1].start()
            index += 1
        for move in moves:
            move.wait_recv()
        if number == 0:

            @pl.when(band == 0)
            def _():
                for m in range(3):
                    band_copy(2, m, 0).start()

        terms = [part[number]] + [got[index - len(stage) + k] for k in range(len(stage))]
        while len(terms) > 1:
            terms = [a + b for a, b in zip(terms[::2], terms[1::2])]
        if number < 2:
            part[number + 1] = terms[0]
        else:
            gram[...] = terms[0]
        for move in moves:
            move.wait_send()

    @pl.when(band == 1)
    def _():
        @pl.loop(0, 3)
        def _(chunk):
            for m in range(3):
                band_copy(chunk, m, 0).wait_recv()
            copy = pltpu.make_async_copy(oth.at[chunk], fo_hbm.at[chunk], out_sem.at[3 + chunk])
            copy.start()
            copy.wait()

    @pl.loop(0, 6)
    def _(slot):
        for m in range(3):
            for copy in copies(slot, m):
                copy.wait_send()
        low_copy(slot).wait_send()
        high_copy(slot).wait_send()

    @pl.loop(0, 3)
    def _(chunk):
        for m in range(3):
            band_copy(chunk, m, 1 - band).wait_send()

            @pl.when(band == 0)
            def _():
                band_copy(chunk, m, 0).wait_send()

        pltpu.make_async_copy(fil.at[chunk], f_hbm.at[chunk], out_sem.at[chunk]).wait()


def filter_call(lines, pot):
    wh, wl = yz_weights()
    sel = face_weights()
    any_space = pl.BlockSpec(memory_space=pl.ANY)
    chunk = (3, CX, 8, CYZ)
    vm = pltpu.VMEM
    return pl.pallas_call(
        filter_kernel,
        out_shape=(
            jax.ShapeDtypeStruct(chunk, F32),
            jax.ShapeDtypeStruct(chunk, F32),
            jax.ShapeDtypeStruct((24, 128), F32),
        ),
        in_specs=[any_space] * 5,
        out_specs=(any_space, any_space, pl.BlockSpec(memory_space=pltpu.VMEM)),
        scratch_shapes=[
            vm((24 * 216, 128), F32),
            vm((216, 128), F32),
            vm(wh.shape, BF),
            vm(wl.shape, BF),
            vm(sel.shape, BF),
            vm((6, CX, 8, LANES), F32),
            vm((6, 6, 8, CYZ), F32),
            vm((6, 6, 8, CYZ), F32),
            vm((6, CX, 8, 384), F32),
            vm((6, CX, 8, 384), F32),
            vm((6, CX, 8, 384), F32),
            vm((6, CX, 8, 384), F32),
            vm((6, 96, LANES), BF),
            vm((6, 96, LANES), BF),
            vm((96, 768), F32),
            vm(chunk, F32),
            vm(chunk, F32),
            vm((3, 24, 128), F32),
            vm((13, 24, 128), F32),
            pltpu.SemaphoreType.DMA((5,)),
            pltpu.SemaphoreType.DMA((6,)),
            pltpu.SemaphoreType.DMA((6, 3, 5)),
            pltpu.SemaphoreType.DMA((6, 3, 5)),
            pltpu.SemaphoreType.DMA((3, 3, 2)),
            pltpu.SemaphoreType.DMA((3, 3, 2)),
            pltpu.SemaphoreType.DMA((13,)),
            pltpu.SemaphoreType.DMA((13,)),
        ],
        compiler_params=pltpu.CompilerParams(collective_id=0, has_side_effects=True, vmem_limit_bytes=56 << 20),
        name="filter",
    )(lines, pot, jnp.asarray(wh), jnp.asarray(wl), jnp.asarray(sel))


def rotate_kernel(low, high, gram, out, mine, theirs, inverse, lines, sems, out_sems):
    band = lax.axis_index("band")

    def loads(x):
        own_load = pltpu.make_async_copy(low.at[:, x], mine.at[:, x], sems.at[0, x])
        return own_load, pltpu.make_async_copy(high.at[:, x], theirs.at[:, x], sems.at[1, x])

    for x in range(CX):
        loads(x)[0].start()

        @pl.when(band == 1)
        def _():
            loads(x)[1].start()

    g = gram[...] * (1.0 / (64 * CX * CYZ))
    blank = jnp.zeros((24, 16), F32)
    row, col = (lax.broadcasted_iota(jnp.int32, (48, 64), d) for d in range(2))
    left = jnp.concatenate(
        [jnp.concatenate([g[:, 0:24], g[:, 96:120], blank], 1), jnp.concatenate([g[:, 64:88], g[:, 32:56], blank], 1)], 0
    )
    table = jnp.concatenate([left, (row == col).astype(F32)], 1)
    rows = lax.broadcasted_iota(jnp.int32, (48, 128), 0)
    for k in range(0, 48, 2):
        one = jnp.broadcast_to(table[:, k : k + 1], (48, 128))
        two = jnp.broadcast_to(table[:, k + 1 : k + 2], (48, 128))
        a, b, c = one[k : k + 1], one[k + 1 : k + 2], two[k + 1 : k + 2]
        upper, lower = table[k : k + 1], table[k + 1 : k + 2]
        inverse[k : k + 1, :] = upper * lax.rsqrt(a)
        ratio = b / a
        inverse[k + 1 : k + 2, :] = (lower - ratio * upper) * lax.rsqrt(c - ratio * b)
        if k < 46:
            scale = 1.0 / (a * c - b * b)
            below = rows > k + 1
            table = (
                table
                - jnp.where(below, one, 0.0) * ((c * upper - b * lower) * scale)
                - jnp.where(below, two, 0.0) * ((a * lower - b * upper) * scale)
            )

    def sent(quarter):
        at = pl.ds(72 * quarter, 72)
        return pltpu.make_async_copy(lines.reshape(24, 216, 128).at[:, at], out.at[:, at], out_sems.at[quarter])

    def rotate(matrix, sources):
        mh, ml = split(matrix)
        left = jnp.concatenate([mh, ml, mh], 1)
        for x in range(CX):
            for load in loads(x)[: len(sources)]:
                load.wait()
            v = [source[:, x].reshape(24, CYZ) for source in sources]
            vh, vl = split(jnp.concatenate(v, 0) if len(v) > 1 else v[0])
            made = dot(left, jnp.concatenate([vh, vh, vl], 0))
            for t in range(18):
                lines[pl.ds(18 * x + t, 24, stride=216), :] = made[:, 128 * t : 128 * t + 128]
            if x % 4 == 3:
                sent(x // 4).start()

    @pl.when(band == 0)
    def _():
        rotate(inverse[0:24, 64:88], [mine])

    @pl.when(band == 1)
    def _():
        rotate(jnp.concatenate([inverse[24:48, 88:112], inverse[24:48, 64:88]], 1), [mine, theirs])

    for quarter in range(3):
        sent(quarter).wait()


def rotate_call(mine, theirs, gram):
    any_space = pl.BlockSpec(memory_space=pl.ANY)
    vm = pltpu.VMEM
    return pl.pallas_call(
        rotate_kernel,
        out_shape=jax.ShapeDtypeStruct((24, 216, 128), F32),
        in_specs=[any_space, any_space, pl.BlockSpec(memory_space=pltpu.VMEM)],
        out_specs=any_space,
        scratch_shapes=[
            vm((3, CX, 8, CYZ), F32),
            vm((3, CX, 8, CYZ), F32),
            vm((48, 128), F32),
            vm((24 * 216, 128), F32),
            pltpu.SemaphoreType.DMA((2, CX)),
            pltpu.SemaphoreType.DMA((3,)),
        ],
        compiler_params=pltpu.CompilerParams(vmem_limit_bytes=56 << 20),
        name="rotate",
    )(mine, theirs, gram)


def body(orbitals, potential):
    mine, theirs, gram = filter_call(orbitals.reshape(24 * 216, 128), potential.reshape(216, 128))
    return rotate_call(mine, theirs, gram).reshape(orbitals.shape)


def solution(mesh):
    return jax.shard_map(
        body,
        mesh=mesh,
        in_specs=(P("band", "dom", None, None), P("dom", None, None)),
        out_specs=P("band", "dom", None, None),
        check_vma=False,
    )
```

```python
import jax
import jax.numpy as jnp
import numpy as np
from jax import lax
from jax.experimental import pallas as pl
from jax.experimental.pallas import tpu as pltpu
from jax.sharding import PartitionSpec as P

CX = 12
CY = 48
CZ = 48
CYZ = CY * CZ
LANES = 3 * 128 + CYZ + 3 * 128
MESH = pl.DeviceIdType.MESH
BF = jnp.bfloat16
F32 = jnp.float32

stencil_weights = (
    -5369.0 / 1800.0,
    12.0 / 7.0,
    -15.0 / 56.0,
    10.0 / 189.0,
    -1.0 / 112.0,
    2.0 / 1925.0,
    -1.0 / 16632.0,
)
centre_shift = 7.25
half_width = 5.25
near = [-0.5 * w / half_width for w in stencil_weights]
own = (-1.5 * stencil_weights[0] - centre_shift) / half_width


def split_np(a):
    a = a.astype(np.float32)
    high = a.astype(BF)
    return high, (a - high.astype(np.float32)).astype(BF)


def yz_weights():
    out = np.zeros((3, 1280, 256), np.float64)
    for part in range(3):
        for n in range(256):
            cell = 256 * part + n
            row, z = cell // CZ, cell % CZ
            for k in range(1, 7):
                for sign in (-1, 1):
                    out[part, n + 384 + sign * CZ * k, n] += near[k]
                    at = z + sign * k
                    if 0 <= at < CZ:
                        out[part, n + 384 + sign * k, n] += near[k]
                    elif at < 0:
                        out[part, 1024 + row * 6 + at + 6, n] += near[k]
                    else:
                        out[part, 1152 + row * 6 + at - CZ, n] += near[k]
    return split_np(out)


def face_weights():
    out = np.zeros((768, 256), np.float32)
    for row in range(16):
        for i in range(6):
            out[row * CZ + i, row * 6 + i] = 1
            out[row * CZ + CZ - 6 + i, 128 + row * 6 + i] = 1
    return out.astype(BF)


def split(v):
    high = v.astype(BF)
    return high, (v - high.astype(F32)).astype(BF)


def dot(a, b):
    return jnp.dot(a, b, preferred_element_type=F32)


def dot_t(a, b):
    return lax.dot_general(a, b, (((1,), (1,)), ((), ())), preferred_element_type=F32)


def flipped(index, bit):
    return index + bit * (1 - 2 * (index // bit % 2))


def filter_kernel(
    orb, pot_hbm, wh_hbm, wl_hbm, sel_hbm, f_hbm, fo_hbm, gram,
    lin, pot, wh, wl, sel, cen, xlo, xhi, zlo, zhi, zlo_out, zhi_out, ylo, yhi, ylo_out, yhi_out, vh, vl, yz, fil, oth, part, got,
    in_sem, out_sem, send_sem, recv_sem, band_send, band_recv, sum_send, sum_recv,
):
    band, dom = lax.axis_index("band"), lax.axis_index("dom")
    pairs = [(orb.at[pl.ds(1728 * c, 1728)], lin.at[pl.ds(1728 * c, 1728)]) for c in range(3)]
    pairs = pairs[:1] + [(sel_hbm, sel), (pot_hbm, pot), (wh_hbm, wh), (wl_hbm, wl)] + pairs[1:]
    loads = [pltpu.make_async_copy(a, b, in_sem.at[i]) for i, (a, b) in enumerate(pairs)]
    for load in loads:
        load.start()

    def across(z, core, y, x, other):
        to = dom
        for bit, used in enumerate((core, z % 2, z // 2, y % 2, y // 2, x)):
            if used:
                to = flipped(to, 1 << bit)
        return (1 - band if other else band), to

    stages = [
        [across(0, 0, 0, k % 2, k // 2) for k in range(1, 4)],
        [across(k // 2, k % 2, 0, 0, 0) for k in range(1, 8)],
        [across(0, 0, k, 0, 0) for k in range(1, 4)],
    ]
    partners = [partner for stage in stages for partner in stage]
    barrier = pltpu.get_barrier_semaphore()
    for partner in partners:
        pl.semaphore_signal(barrier, 1, device_id=partner, device_id_type=MESH)

    ends = []
    for first in (1, 4, 16):
        odd = (dom // first % 4 + 1) // 2 % 2
        below = odd * flipped(dom, first) + (1 - odd) * flipped(dom, 2 * first)
        above = odd * flipped(dom, 2 * first) + (1 - odd) * flipped(dom, first)
        ends.append(((band, below), (band, above)))

    def copies(slot, m):
        lanes, centre, face = pl.ds(768 * m, 768), pl.ds(384 + 768 * m, 768), pl.ds(128 * m, 128)
        table = (
            (cen.at[slot, pl.ds(0, 6), :, centre], xhi.at[slot, :, :, lanes], ends[0][0]),
            (cen.at[slot, pl.ds(6, 6), :, centre], xlo.at[slot, :, :, lanes], ends[0][1]),
            (zlo_out.at[slot, :, :, face], zhi.at[slot, :, :, face], ends[2][0]),
            (zhi_out.at[slot, :, :, face], zlo.at[slot, :, :, face], ends[2][1]),
        )
        return [
            pltpu.make_async_remote_copy(
                a, b, send_sem.at[slot, m, i], recv_sem.at[slot, m, i], device_id=to, device_id_type=MESH
            )
            for i, (a, b, to) in enumerate(table)
        ]

    def y_copies(slot, m):
        if m == 0:
            table = ((cen.at[slot, :, :, pl.ds(384, 256)], cen.at[slot, :, :, pl.ds(384 + CYZ, 256)]), (ylo_out, yhi))
        else:
            table = ((cen.at[slot, :, :, pl.ds(128 + CYZ, 256)], cen.at[slot, :, :, pl.ds(128, 256)]), (yhi_out, ylo))
        table = (table[0], (table[1][0].at[slot], table[1][1].at[slot]))
        return [
            pltpu.make_async_remote_copy(
                a, b, send_sem.at[slot, m, 4 + i], recv_sem.at[slot, m, 4 + i],
                device_id=ends[1][m // 2], device_id_type=MESH,
            )
            for i, (a, b) in enumerate(table)
        ]

    def band_copy(chunk, m, half):
        part_of = (chunk, pl.ds(6 * half, 6), slice(None), pl.ds(768 * m, 768))
        return pltpu.make_async_remote_copy(
            fil.at[part_of], oth.at[part_of], band_send.at[chunk, m, half], band_recv.at[chunk, m, half],
            device_id=(1 - band, dom), device_id_type=MESH,
        )

    lane = lax.broadcasted_iota(jnp.int32, (8, 128), 1)

    def group(i):
        return 2 * i % 3

    def prepare(slot, m):
        lanes = pl.ds(pl.multiple_of(384 + 768 * m, 128), 768)
        face = pl.ds(pl.multiple_of(128 * m, 128), 128)
        high, low = split(cen[slot, :, :, lanes].reshape(96, 768))
        vh[slot, :, lanes] = high
        vl[slot, :, lanes] = low
        faces = dot(high, sel[...]) + dot(low, sel[...])
        for out, at in ((zlo_out, 0), (zhi_out, 128)):
            f = faces[:, at : at + 128].reshape(CX, 8, 128)
            for x in range(9):
                last = pltpu.roll(f[x // 3 * 4 + 3], 96 - 32 * (x % 3), 1)
                out[slot, x, :, face] = jnp.where(lane < 96, f[x // 3 * 4 + x % 3], last)
        for copy in copies(slot, m):
            copy.start()

        def y_face(m, out, start, shift):
            for g in range(3):
                v = [cen[slot, 4 * g + q, :, pl.ds(start, 128)] for q in range(4)]
                v = [pltpu.roll(v[q], (32 * q + shift) % 128, 1) for q in range(4)]
                out[slot, g] = jnp.where(
                    lane < 64, jnp.where(lane < 32, v[0], v[1]), jnp.where(lane < 96, v[2], v[3])
                )
            for copy in y_copies(slot, m):
                copy.start()

        @pl.when(m == 0)
        def _():
            y_face(0, ylo_out, 640, 0)

        @pl.when(m == 2)
        def _():
            y_face(2, yhi_out, CYZ, 32)

    def split_rim(slot, m, packed, start, at, shift):
        for copy in y_copies(slot, m):
            copy.wait_recv()
        for x in range(CX):
            cen[slot, x, :, pl.ds(at, 128)] = pltpu.roll(packed[slot, x // 4], (shift - 32 * (x % 4)) % 128, 1)
        high, low = split(cen[slot, :, :, pl.ds(start, 384)].reshape(96, 384))
        vh[slot, :, pl.ds(start, 384)] = high
        vl[slot, :, pl.ds(start, 384)] = low

    def receive(slot, m):
        for copy in copies(slot, m):
            copy.wait_recv()

        @pl.when(m == 0)
        def _():
            split_rim(slot, 2, ylo, 0, 0, 96)

        @pl.when(m == 2)
        def _():
            split_rim(slot, 0, yhi, 384 + CYZ, 640 + CYZ, 0)

    def z_rim(rim, slot, face):
        out = []
        for g in range(3):
            v = [rim[slot, 3 * g + q, :, face] for q in range(3)]
            r = [pltpu.roll(v[q], 32 + 32 * q, 1) for q in range(3)]
            out += v + [jnp.where(lane < 32, r[0], jnp.where(lane < 64, r[1], r[2]))]
        return jnp.concatenate(out, 0)

    def yz_product(slot, m):
        face = pl.ds(pl.multiple_of(128 * m, 128), 128)
        rims = jnp.concatenate([z_rim(zlo, slot, face), z_rim(zhi, slot, face)], 1)
        zh, zl = split(rims)
        for j in range(3):
            window = pl.ds(pl.multiple_of(256 * j + 768 * m, 256), 1024)
            high = jnp.concatenate([vh[slot, :, window], zh], 1)
            low = jnp.concatenate([vl[slot, :, window], zl], 1)
            yz[:, pl.ds(256 * j, 256)] = dot(high, wh[j]) + dot(low, wh[j]) + dot(high, wl[j])

    def stencil(slot, m, write):
        @pl.loop(0, 6)
        def _(t):
            at = pl.multiple_of(768 * m + 128 * t, 128)
            here, mid = pl.ds(at, 128), pl.ds(pl.multiple_of(at + 384, 128), 128)
            v = [xlo[slot, i, :, here] for i in range(6)]
            v += [cen[slot, i, :, mid] for i in range(CX)]
            v += [xhi[slot, i, :, here] for i in range(6)]
            for x in range(CX):
                diagonal = pot[pl.ds(18 * x + 6 * m + t, 1), :] * (1.0 / half_width) + own
                total = diagonal * v[x + 6] + yz[pl.ds(8 * x, 8), pl.ds(pl.multiple_of(128 * t, 128), 128)]
                for k in range(1, 7):
                    total = total + near[k] * (v[x + 6 - k] + v[x + 6 + k])
                write(x, here, mid, total)

    def relayout(chunk, m):
        for x in range(CX):
            for t in range(6):
                row = 8 * 216 * chunk + 18 * x + 6 * m + t
                lanes = pl.ds(pl.multiple_of(384 + 768 * m + 128 * t, 128), 128)
                cen[chunk, x, :, lanes] = lin[pl.ds(row, 8, stride=216), :]

    def rows(ref, m, first, layers):
        lanes = pl.ds(pl.multiple_of(768 * m, 128), 768)
        pieces = [split(ref[:, first + x, :, lanes].reshape(24, 768)) for x in range(layers)]
        return jnp.concatenate([jnp.concatenate([p[i] for p in pieces], 1) for i in range(2)], 0)

    def folded(a, b):
        products = dot_t(a, b)
        return products[:24, :24] + products[24:, :24] + products[:24, 24:]

    def own_products(m):
        a = rows(fil, m, 0, CX)
        part[0, :, 0:24] += folded(a, a)

    def enter(chunk, m):
        relayout(chunk, m)
        prepare(chunk, m)

    part[0] = jnp.zeros((24, 128), F32)
    loads[0].wait()
    loads[1].wait()
    pl.semaphore_wait(barrier, len(partners))

    @pl.loop(0, 3)
    def _(i):
        enter(0, group(i))

    for load in loads[2:]:
        load.wait()

    @pl.loop(0, 3)
    def _(chunk):
        @pl.loop(0, 3)
        def _(i):
            m = group(i)
            receive(chunk, m)

            def write(x, here, mid, total):
                cen[chunk + 3, x, :, mid] = total

            yz_product(chunk, m)
            stencil(chunk, m, write)
            prepare(chunk + 3, m)

        @pl.loop(0, 3)
        def _(i):
            m = group(i)
            receive(chunk + 3, m)

            @pl.when(chunk < 2)
            def _():
                enter(chunk + 1, m)

            def write(x, here, mid, total):
                fil[chunk, x, :, here] = 2.0 * total - cen[chunk, x, :, mid]

            yz_product(chunk + 3, m)
            stencil(chunk + 3, m, write)
            band_copy(chunk, m, 1 - band).start()

            @pl.when((band == 0) & (chunk < 2))
            def _():
                band_copy(chunk, m, 0).start()

            @pl.when(chunk == 2)
            def _():
                own_products(m)

        pltpu.make_async_copy(fil.at[chunk], f_hbm.at[chunk], out_sem.at[chunk]).start()

    part[0] = jnp.where(band == 0, part[0], pltpu.roll(part[0], 32, 1))

    @pl.loop(0, 3)
    def _(i):
        m = group(i)
        for chunk in range(3):
            band_copy(chunk, m, band).wait_recv()

        mine, theirs = rows(fil, m, 6 * band, 6), rows(oth, m, 6 * band, 6)
        first, second = jnp.where(band == 0, mine, theirs), jnp.where(band == 0, theirs, mine)
        part[0, :, 64:88] += folded(second, first)
        part[0, :, 96:120] += folded(first, second)

    index = 0
    for number, stage in enumerate(stages):
        moves = []
        for partner in stage:
            moves.append(
                pltpu.make_async_remote_copy(
                    part.at[number], got.at[index], sum_send.at[index], sum_recv.at[index],
                    device_id=partner, device_id_type=MESH,
                )
            )
            moves[-1].start()
            index += 1
        for move in moves:
            move.wait_recv()
        if number == 0:

            @pl.when(band == 0)
            def _():
                for m in range(3):
                    band_copy(2, m, 0).start()

        terms = [part[number]] + [got[index - len(stage) + k] for k in range(len(stage))]
        while len(terms) > 1:
            terms = [a + b for a, b in zip(terms[::2], terms[1::2])]
        if number < 2:
            part[number + 1] = terms[0]
        else:
            gram[...] = terms[0]
        for move in moves:
            move.wait_send()

    @pl.when(band == 1)
    def _():
        @pl.loop(0, 3)
        def _(chunk):
            for m in range(3):
                band_copy(chunk, m, 0).wait_recv()
            copy = pltpu.make_async_copy(oth.at[chunk], fo_hbm.at[chunk], out_sem.at[3 + chunk])
            copy.start()
            copy.wait()

    @pl.loop(0, 6)
    def _(slot):
        for m in range(3):
            for copy in copies(slot, m):
                copy.wait_send()
        for copy in y_copies(slot, 0) + y_copies(slot, 2):
            copy.wait_send()

    @pl.loop(0, 3)
    def _(chunk):
        for m in range(3):
            band_copy(chunk, m, 1 - band).wait_send()

            @pl.when(band == 0)
            def _():
                band_copy(chunk, m, 0).wait_send()

        pltpu.make_async_copy(fil.at[chunk], f_hbm.at[chunk], out_sem.at[chunk]).wait()


def filter_call(lines, pot):
    wh, wl = yz_weights()
    sel = face_weights()
    any_space = pl.BlockSpec(memory_space=pl.ANY)
    chunk = (3, CX, 8, CYZ)
    vm = pltpu.VMEM
    return pl.pallas_call(
        filter_kernel,
        out_shape=(
            jax.ShapeDtypeStruct(chunk, F32),
            jax.ShapeDtypeStruct(chunk, F32),
            jax.ShapeDtypeStruct((24, 128), F32),
        ),
        in_specs=[any_space] * 5,
        out_specs=(any_space, any_space, pl.BlockSpec(memory_space=pltpu.VMEM)),
        scratch_shapes=[
            vm((24 * 216, 128), F32),
            vm((216, 128), F32),
            vm(wh.shape, BF),
            vm(wl.shape, BF),
            vm(sel.shape, BF),
            vm((6, CX, 8, LANES), F32),
            vm((6, 6, 8, CYZ), F32),
            vm((6, 6, 8, CYZ), F32),
            vm((6, 9, 8, 384), F32),
            vm((6, 9, 8, 384), F32),
            vm((6, 9, 8, 384), F32),
            vm((6, 9, 8, 384), F32),
            vm((6, 3, 8, 128), F32),
            vm((6, 3, 8, 128), F32),
            vm((6, 3, 8, 128), F32),
            vm((6, 3, 8, 128), F32),
            vm((6, 96, LANES), BF),
            vm((6, 96, LANES), BF),
            vm((96, 768), F32),
            vm(chunk, F32),
            vm(chunk, F32),
            vm((3, 24, 128), F32),
            vm((13, 24, 128), F32),
            pltpu.SemaphoreType.DMA((7,)),
            pltpu.SemaphoreType.DMA((6,)),
            pltpu.SemaphoreType.DMA((6, 3, 6)),
            pltpu.SemaphoreType.DMA((6, 3, 6)),
            pltpu.SemaphoreType.DMA((3, 3, 2)),
            pltpu.SemaphoreType.DMA((3, 3, 2)),
            pltpu.SemaphoreType.DMA((13,)),
            pltpu.SemaphoreType.DMA((13,)),
        ],
        compiler_params=pltpu.CompilerParams(collective_id=0, has_side_effects=True, vmem_limit_bytes=56 << 20),
        name="filter",
    )(lines, pot, jnp.asarray(wh), jnp.asarray(wl), jnp.asarray(sel))


def rotate_kernel(low, high, gram, out, mine, theirs, inverse, lines, sems, out_sems):
    band = lax.axis_index("band")

    def loads(x):
        own_load = pltpu.make_async_copy(low.at[:, x], mine.at[:, x], sems.at[0, x])
        return own_load, pltpu.make_async_copy(high.at[:, x], theirs.at[:, x], sems.at[1, x])

    for x in range(CX):
        loads(x)[0].start()

        @pl.when(band == 1)
        def _():
            loads(x)[1].start()

    g = gram[...] * (1.0 / (64 * CX * CYZ))
    blank = jnp.zeros((24, 16), F32)
    row, col = (lax.broadcasted_iota(jnp.int32, (48, 64), d) for d in range(2))
    left = jnp.concatenate(
        [jnp.concatenate([g[:, 0:24], g[:, 96:120], blank], 1), jnp.concatenate([g[:, 64:88], g[:, 32:56], blank], 1)], 0
    )
    table = jnp.concatenate([left, (row == col).astype(F32)], 1)
    rows = lax.broadcasted_iota(jnp.int32, (48, 128), 0)
    for k in range(0, 48, 2):
        one = jnp.broadcast_to(table[:, k : k + 1], (48, 128))
        two = jnp.broadcast_to(table[:, k + 1 : k + 2], (48, 128))
        a, b, c = one[k : k + 1], one[k + 1 : k + 2], two[k + 1 : k + 2]
        upper, lower = table[k : k + 1], table[k + 1 : k + 2]
        inverse[k : k + 1, :] = upper * lax.rsqrt(a)
        ratio = b / a
        inverse[k + 1 : k + 2, :] = (lower - ratio * upper) * lax.rsqrt(c - ratio * b)
        if k < 46:
            scale = 1.0 / (a * c - b * b)
            below = rows > k + 1
            table = (
                table
                - jnp.where(below, one, 0.0) * ((c * upper - b * lower) * scale)
                - jnp.where(below, two, 0.0) * ((a * lower - b * upper) * scale)
            )

    def sent(quarter):
        at = pl.ds(72 * quarter, 72)
        return pltpu.make_async_copy(lines.reshape(24, 216, 128).at[:, at], out.at[:, at], out_sems.at[quarter])

    def rotate(matrix, sources):
        mh, ml = split(matrix)
        left = jnp.concatenate([mh, ml, mh], 1)
        for x in range(CX):
            for load in loads(x)[: len(sources)]:
                load.wait()
            v = [source[:, x].reshape(24, CYZ) for source in sources]
            vh, vl = split(jnp.concatenate(v, 0) if len(v) > 1 else v[0])
            made = dot(left, jnp.concatenate([vh, vh, vl], 0))
            for t in range(18):
                lines[pl.ds(18 * x + t, 24, stride=216), :] = made[:, 128 * t : 128 * t + 128]
            if x % 4 == 3:
                sent(x // 4).start()

    @pl.when(band == 0)
    def _():
        rotate(inverse[0:24, 64:88], [mine])

    @pl.when(band == 1)
    def _():
        rotate(jnp.concatenate([inverse[24:48, 88:112], inverse[24:48, 64:88]], 1), [mine, theirs])

    for quarter in range(3):
        sent(quarter).wait()


def rotate_call(mine, theirs, gram):
    any_space = pl.BlockSpec(memory_space=pl.ANY)
    vm = pltpu.VMEM
    return pl.pallas_call(
        rotate_kernel,
        out_shape=jax.ShapeDtypeStruct((24, 216, 128), F32),
        in_specs=[any_space, any_space, pl.BlockSpec(memory_space=pltpu.VMEM)],
        out_specs=any_space,
        scratch_shapes=[
            vm((3, CX, 8, CYZ), F32),
            vm((3, CX, 8, CYZ), F32),
            vm((48, 128), F32),
            vm((24 * 216, 128), F32),
            pltpu.SemaphoreType.DMA((2, CX)),
            pltpu.SemaphoreType.DMA((3,)),
        ],
        compiler_params=pltpu.CompilerParams(vmem_limit_bytes=56 << 20),
        name="rotate",
    )(mine, theirs, gram)


def body(orbitals, potential):
    mine, theirs, gram = filter_call(orbitals.reshape(24 * 216, 128), potential.reshape(216, 128))
    return rotate_call(mine, theirs, gram).reshape(orbitals.shape)


def solution(mesh):
    return jax.shard_map(
        body,
        mesh=mesh,
        in_specs=(P("band", "dom", None, None), P("dom", None, None)),
        out_specs=P("band", "dom", None, None),
        check_vma=False,
    )
```

```python
import jax
import jax.numpy as jnp
import numpy as np
from jax import lax
from jax.experimental import pallas as pl
from jax.experimental.pallas import tpu as pltpu
from jax.sharding import PartitionSpec as P

CX = 12
CY = 48
CZ = 48
CYZ = CY * CZ
LANES = 3 * 128 + CYZ + 3 * 128
MESH = pl.DeviceIdType.MESH
BF = jnp.bfloat16
F32 = jnp.float32

stencil_weights = (
    -5369.0 / 1800.0,
    12.0 / 7.0,
    -15.0 / 56.0,
    10.0 / 189.0,
    -1.0 / 112.0,
    2.0 / 1925.0,
    -1.0 / 16632.0,
)
centre_shift = 7.25
half_width = 5.25
near = [-0.5 * w / half_width for w in stencil_weights]
own = (-1.5 * stencil_weights[0] - centre_shift) / half_width


def split_np(a):
    a = a.astype(np.float32)
    high = a.astype(BF)
    return high, (a - high.astype(np.float32)).astype(BF)


def yz_weights():
    out = np.zeros((3, 1280, 256), np.float64)
    for part in range(3):
        for n in range(256):
            cell = 256 * part + n
            row, z = cell // CZ, cell % CZ
            for k in range(1, 7):
                for sign in (-1, 1):
                    out[part, n + 384 + sign * CZ * k, n] += near[k]
                    at = z + sign * k
                    if 0 <= at < CZ:
                        out[part, n + 384 + sign * k, n] += near[k]
                    elif at < 0:
                        out[part, 1024 + row * 6 + at + 6, n] += near[k]
                    else:
                        out[part, 1152 + row * 6 + at - CZ, n] += near[k]
    return split_np(out)


def face_weights():
    out = np.zeros((768, 256), np.float32)
    for row in range(16):
        for i in range(6):
            out[row * CZ + i, row * 6 + i] = 1
            out[row * CZ + CZ - 6 + i, 128 + row * 6 + i] = 1
    return out.astype(BF)


def split(v):
    high = v.astype(BF)
    return high, (v - high.astype(F32)).astype(BF)


def dot(a, b):
    return jnp.dot(a, b, preferred_element_type=F32)


def dot_t(a, b):
    return lax.dot_general(a, b, (((1,), (1,)), ((), ())), preferred_element_type=F32)


def flipped(index, bit):
    return index + bit * (1 - 2 * (index // bit % 2))


def filter_kernel(
    orb, pot_hbm, wh_hbm, wl_hbm, sel_hbm, f_hbm, fo_hbm, gram,
    lin, pot, wh, wl, sel, cen, xrim, zlo, zhi, zlo_out, zhi_out, ylo, yhi, ylo_out, yhi_out, passed, vh, vl, yz, fil, oth, relay, part, got,
    in_sem, out_sem, send_sem, recv_sem, y_send, y_recv, pass_send, hop_send, hop_recv, band_send, band_recv, sum_send, sum_recv,
):
    band, dom = lax.axis_index("band"), lax.axis_index("dom")
    pairs = [(orb.at[pl.ds(1728 * c, 1728)], lin.at[pl.ds(1728 * c, 1728)]) for c in range(3)]
    pairs = pairs[:1] + [(sel_hbm, sel), (pot_hbm, pot), (wh_hbm, wh), (wl_hbm, wl)] + pairs[1:]
    loads = [pltpu.make_async_copy(a, b, in_sem.at[i]) for i, (a, b) in enumerate(pairs)]
    for load in loads:
        load.start()

    def across(z, core, y, x, other):
        to = dom
        for bit, used in enumerate((core, z % 2, z // 2, y % 2, y // 2, x)):
            if used:
                to = flipped(to, 1 << bit)
        return (1 - band if other else band), to

    stages = [
        [across(k // 2, k % 2, 0, 0, 0) for k in range(1, 8)],
        [across(0, 0, k // 4, k // 2 % 2, k % 2) for k in range(1, 16)],
    ]
    partners = [partner for stage in stages for partner in stage]
    barrier = pltpu.get_barrier_semaphore()
    for partner in partners:
        pl.semaphore_signal(barrier, 1, device_id=partner, device_id_type=MESH)

    ends, odds = [], []
    for first in (1, 4, 16):
        odd = (dom // first % 4 + 1) // 2 % 2
        below = odd * flipped(dom, first) + (1 - odd) * flipped(dom, 2 * first)
        above = odd * flipped(dom, 2 * first) + (1 - odd) * flipped(dom, first)
        ends.append(((band, below), (band, above)))
        odds.append(odd)

    def copies(slot, m):
        face = pl.ds(128 * m, 128)
        table = []
        for part in range(2):
            start = 768 * m + 384 * (part * odds[1] + (1 - part) * (1 - odds[1]))
            lanes, centre = pl.ds(start, 384), pl.ds(384 + start, 384)
            table += [
                (cen.at[slot, pl.ds(0, 6), :, centre], xrim.at[slot, 1, :, :, lanes], ends[0][0]),
                (cen.at[slot, pl.ds(6, 6), :, centre], xrim.at[slot, 0, :, :, lanes], ends[0][1]),
            ]
        table += [
            (zlo_out.at[slot, :, :, face], zhi.at[slot, :, :, face], ends[2][0]),
            (zhi_out.at[slot, :, :, face], zlo.at[slot, :, :, face], ends[2][1]),
        ]
        return [
            pltpu.make_async_remote_copy(
                a, b, send_sem.at[slot, m, i], recv_sem.at[slot, m, i], device_id=to, device_id_type=MESH
            )
            for i, (a, b, to) in enumerate(table)
        ]

    def y_moves(slot, face, half, sources, sems, to):
        rim = cen.at[slot, pl.ds(6 * half, 6), :, pl.ds((384 + CYZ, 128)[face], 256)]
        return [
            pltpu.make_async_remote_copy(
                a, b, sems[i], y_recv.at[slot, face, half, i], device_id=to, device_id_type=MESH
            )
            for i, (a, b) in enumerate(zip(sources, (rim, (yhi, ylo)[face].at[slot, half])))
        ]

    def y_copies(slot, face, half):
        sources = (
            cen.at[slot, pl.ds(6 * half, 6), :, pl.ds((384, 128 + CYZ)[face], 256)],
            (ylo_out, yhi_out)[face].at[slot, half],
        )
        sems = [y_send.at[slot, face, half, i] for i in range(2)]
        return y_moves(slot, face, half, sources, sems, ends[1][face])

    def forward_copies(slot, face):
        sources = (xrim.at[slot, odds[0], :, :, pl.ds((0, CYZ - 256)[face], 256)], passed.at[slot])
        sems = [pass_send.at[slot, i] for i in range(2)]
        return y_moves(slot, face, 1 - odds[0], sources, sems, (band, flipped(flipped(dom, 2), 4)))

    def band_copy(chunk, m, half):
        part_of = (chunk, pl.ds(6 * half, 6), slice(None), pl.ds(768 * m, 768))
        return pltpu.make_async_remote_copy(
            fil.at[part_of], oth.at[part_of], band_send.at[chunk, m, half], band_recv.at[chunk, m, half],
            device_id=(1 - band, dom), device_id_type=MESH,
        )

    far, near_by = (1 - band, flipped(dom, 32)), (1 - band, dom)

    def hop(a, b, number, chunk, m, to):
        return pltpu.make_async_remote_copy(
            a, b, hop_send.at[number, chunk, m], hop_recv.at[number, chunk, m], device_id=to, device_id_type=MESH
        )

    def hops(number, chunk):
        if number == 0:
            return [
                first_hop(chunk, m)
                for m in range(3)
            ]
        if number == 1:
            return [hop(relay.at[chunk], relay.at[chunk], 1, chunk, 0, near_by)]
        return [hop(relay.at[chunk], oth.at[chunk, pl.ds(0, 6)], 2, chunk, 0, far)]

    def first_hop(chunk, m):
        at = pl.ds(pl.multiple_of(768 * m, 128), 768)
        return hop(fil.at[chunk, pl.ds(0, 6), :, at], relay.at[chunk, :, :, at], 0, chunk, m, far)

    def pass_on(number, chunk):
        @pl.when(band == 2 - number)
        def _():
            for copy in hops(number - 1, chunk):
                copy.wait_recv()
            for copy in hops(number, chunk):
                copy.start()

    lane = lax.broadcasted_iota(jnp.int32, (8, 128), 1)

    def group(i):
        return 2 - i + odds[1] * (2 * i - 2)

    def packed(tiles, shift):
        v = [pltpu.roll(tile, (32 * (q % 4) + shift) % 128, 1) for q, tile in enumerate(tiles)]
        first = jnp.where(lane < 64, jnp.where(lane < 32, v[0], v[1]), jnp.where(lane < 96, v[2], v[3]))
        return first, jnp.where(lane < 32, v[4], v[5])

    def for_outer(face, act):
        @pl.when(odds[1] == face)
        def _():
            act()

    def send_y(slot, face):
        start, shift = ((640, 0), (CYZ, 32))[face]
        for half in range(2):
            tiles = [cen[slot, 6 * half + q, :, pl.ds(start, 128)] for q in range(6)]
            out = (ylo_out, yhi_out)[face]
            out[slot, half, 0], out[slot, half, 1] = packed(tiles, shift)

        def start_outer():
            for copy in y_copies(slot, face, odds[0]):
                copy.start()

        for copy in y_copies(slot, face, 1 - odds[0]):
            copy.start()
        for_outer(face, start_outer)

    def forward(slot):
        for face in range(2):

            @pl.when(odds[1] == 1 - face)
            def _():
                start, shift = ((256, 0), (CYZ - 384, 32))[face]
                tiles = [xrim[slot, odds[0], q, :, pl.ds(start, 128)] for q in range(6)]
                passed[slot, 0], passed[slot, 1] = packed(tiles, shift)
                for copy in forward_copies(slot, face):
                    copy.start()

    def prepare(slot, m):
        lanes = pl.ds(pl.multiple_of(384 + 768 * m, 128), 768)
        face = pl.ds(pl.multiple_of(128 * m, 128), 128)
        high, low = split(cen[slot, :, :, lanes].reshape(96, 768))
        vh[slot, :, lanes] = high
        vl[slot, :, lanes] = low
        faces = dot(high, sel[...]) + dot(low, sel[...])
        for out, at in ((zlo_out, 0), (zhi_out, 128)):
            f = faces[:, at : at + 128].reshape(CX, 8, 128)
            for x in range(9):
                last = pltpu.roll(f[x // 3 * 4 + 3], 96 - 32 * (x % 3), 1)
                out[slot, x, :, face] = jnp.where(lane < 96, f[x // 3 * 4 + x % 3], last)

    def send(slot, m, first, count):
        for copy in copies(slot, m)[first : first + count]:
            copy.start()

    def split_rim(slot, face, rim, start, at, shift):
        for half in range(2):
            for copy in y_copies(slot, face, half):
                copy.wait_recv()
        for x in range(CX):
            tile = rim[slot, x // 6, x % 6 // 4]
            cen[slot, x, :, pl.ds(at, 128)] = pltpu.roll(tile, (shift - 32 * (x % 6 % 4)) % 128, 1)
        high, low = split(cen[slot, :, :, pl.ds(start, 384)].reshape(96, 384))
        vh[slot, :, pl.ds(start, 384)] = high
        vl[slot, :, pl.ds(start, 384)] = low

    def receive_y(slot, m):
        @pl.when(m == 0)
        def _():
            split_rim(slot, 1, ylo, 0, 0, 96)

        @pl.when(m == 2)
        def _():
            split_rim(slot, 0, yhi, 384 + CYZ, 640 + CYZ, 0)

    def receive(slot, m, first, count):
        for copy in copies(slot, m)[first : first + count]:
            copy.wait_recv()

    def arrive(slot, m, i):
        @pl.when(i == 0)
        def _():
            receive(slot, m, 0, 2)
            forward(slot)

        receive_y(slot, m)
        yz_product(slot, m)

        @pl.when(i > 0)
        def _():
            receive(slot, m, 0, 2)

        receive(slot, m, 2, 4)

    def z_rim(rim, slot, face):
        out = []
        for g in range(3):
            v = [rim[slot, 3 * g + q, :, face] for q in range(3)]
            r = [pltpu.roll(v[q], 32 + 32 * q, 1) for q in range(3)]
            out += v + [jnp.where(lane < 32, r[0], jnp.where(lane < 64, r[1], r[2]))]
        return jnp.concatenate(out, 0)

    def yz_product(slot, m):
        for j in range(3):
            window = pl.ds(pl.multiple_of(256 * j + 768 * m, 256), 1024)
            high, low = vh[slot, :, window], vl[slot, :, window]
            wide = dot(high, wh[j, 0:1024]) + dot(low, wh[j, 0:1024]) + dot(high, wl[j, 0:1024])
            yz[:, pl.ds(256 * j, 256)] = wide

    def rim_product(slot, m):
        face = pl.ds(pl.multiple_of(128 * m, 128), 128)
        high, low = split(jnp.concatenate([z_rim(zlo, slot, face), z_rim(zhi, slot, face)], 1))
        for j in range(3):
            rims = slice(1024, 1280)
            yz[:, pl.ds(256 * j, 256)] += dot(high, wh[j, rims]) + dot(low, wh[j, rims]) + dot(high, wl[j, rims])

    def stencil(slot, m, write):
        @pl.loop(0, 6)
        def _(t):
            at = pl.multiple_of(768 * m + 128 * t, 128)
            here, mid = pl.ds(at, 128), pl.ds(pl.multiple_of(at + 384, 128), 128)
            v = [xrim[slot, 0, i, :, here] for i in range(6)]
            v += [cen[slot, i, :, mid] for i in range(CX)]
            v += [xrim[slot, 1, i, :, here] for i in range(6)]
            for x in range(CX):
                diagonal = pot[pl.ds(18 * x + 6 * m + t, 1), :] * (1.0 / half_width) + own
                total = diagonal * v[x + 6] + yz[pl.ds(8 * x, 8), pl.ds(pl.multiple_of(128 * t, 128), 128)]
                for k in range(1, 7):
                    total = total + near[k] * (v[x + 6 - k] + v[x + 6 + k])
                write(x, here, mid, total)

    def relayout(chunk, m):
        for x in range(CX):
            for t in range(6):
                row = 8 * 216 * chunk + 18 * x + 6 * m + t
                lanes = pl.ds(pl.multiple_of(384 + 768 * m + 128 * t, 128), 128)
                cen[chunk, x, :, lanes] = lin[pl.ds(row, 8, stride=216), :]

    def rows(ref, m, first, layers):
        lanes = pl.ds(pl.multiple_of(768 * m, 128), 768)
        pieces = [split(ref[:, first + x, :, lanes].reshape(24, 768)) for x in range(layers)]
        return jnp.concatenate([jnp.concatenate([p[i] for p in pieces], 1) for i in range(2)], 0)

    def folded(a, b):
        products = dot_t(a, b)
        return products[:24, :24] + products[24:, :24] + products[:24, 24:]

    def own_products(m):
        a = rows(fil, m, 0, CX)
        part[0, :, 0:24] += folded(a, a)

    def enter(chunk):
        @pl.loop(0, 3)
        def _(i):
            relayout(chunk, group(i))

    part[0] = jnp.zeros((24, 128), F32)
    loads[0].wait()
    loads[1].wait()
    pl.semaphore_wait(barrier, len(partners))
    enter(0)
    send(0, group(0), 0, 4)
    send_y(0, 0)
    send_y(0, 1)

    @pl.loop(0, 3)
    def _(i):
        @pl.when(i > 0)
        def _():
            send(0, group(i), 0, 4)

        prepare(0, group(i))
        send(0, group(i), 4, 2)

    for load in loads[2:]:
        load.wait()

    @pl.loop(0, 3)
    def _(chunk):
        @pl.loop(0, 3)
        def _(i):
            m, slot = group(i), chunk
            arrive(slot, m, i)
            rim_product(slot, m)

            def write(x, here, mid, total):
                cen[chunk + 3, x, :, mid] = total

            stencil(slot, m, write)

            send(slot + 3, m, 0, 4)

            @pl.when(m == 0)
            def _():
                send_y(slot + 3, 0)

            @pl.when(m == 2)
            def _():
                send_y(slot + 3, 1)

            prepare(slot + 3, m)
            send(slot + 3, m, 4, 2)

        @pl.when(chunk > 0)
        def _():
            pass_on(1, chunk - 1)

        @pl.when(chunk < 2)
        def _():
            enter(chunk + 1)
            send_y(chunk + 1, 0)
            send_y(chunk + 1, 1)

            @pl.loop(0, 3)
            def _(i):
                prepare(chunk + 1, group(i))

        @pl.loop(0, 3)
        def _(i):
            m, slot = group(i), chunk + 3
            arrive(slot, m, i)

            @pl.when(chunk < 2)
            def _():
                send(chunk + 1, m, 0, 6)

            rim_product(slot, m)

            def write(x, here, mid, total):
                fil[chunk, x, :, here] = 2.0 * total - cen[chunk, x, :, mid]

            stencil(slot, m, write)
            band_copy(chunk, m, 1 - band).start()

            @pl.when((band == 0) & (chunk < 2))
            def _():
                first_hop(chunk, m).start()

            @pl.when(chunk == 2)
            def _():
                own_products(m)

        pltpu.make_async_copy(fil.at[chunk], f_hbm.at[chunk], out_sem.at[chunk]).start()

        @pl.when(chunk > 0)
        def _():
            pass_on(2, chunk - 1)

    part[0] = jnp.where(band == 0, part[0], pltpu.roll(part[0], 32, 1))

    def cross_products(m):
        for chunk in range(3):
            band_copy(chunk, m, band).wait_recv()
        mine, theirs = rows(fil, m, 6 * band, 6), rows(oth, m, 6 * band, 6)
        first, second = jnp.where(band == 0, mine, theirs), jnp.where(band == 0, theirs, mine)
        part[0, :, 64:88] += folded(second, first)
        part[0, :, 96:120] += folded(first, second)

    @pl.loop(0, 3)
    def _(i):
        @pl.when(i == 2)
        def _():
            for m in range(3):
                band_copy(2, m, 1 - band).wait_send()

            @pl.when(band == 0)
            def _():
                for m in range(3):
                    band_copy(2, m, 0).start()

        cross_products(group(i))

    index = 0
    for number, stage in enumerate(stages):
        moves = []
        for partner in stage:
            moves.append(
                pltpu.make_async_remote_copy(
                    part.at[number], got.at[index], sum_send.at[index], sum_recv.at[index],
                    device_id=partner, device_id_type=MESH,
                )
            )
            moves[-1].start()
            index += 1
        for move in moves:
            move.wait_recv()
        terms = [part[number]] + [got[index - len(stage) + k] for k in range(len(stage))]
        while len(terms) > 1:
            terms = [a + b for a, b in zip(terms[::2], terms[1::2])]
        if number < 1:
            part[number + 1] = terms[0]
        else:
            gram[...] = terms[0]
        for move in moves:
            move.wait_send()

    @pl.when(band == 1)
    def _():
        @pl.loop(0, 3)
        def _(chunk):
            @pl.when(chunk < 2)
            def _():
                for copy in hops(2, chunk):
                    copy.wait_recv()
                for copy in hops(1, chunk):
                    copy.wait_send()

            @pl.when(chunk == 2)
            def _():
                for m in range(3):
                    band_copy(2, m, 0).wait_recv()

            copy = pltpu.make_async_copy(oth.at[chunk], fo_hbm.at[chunk], out_sem.at[3 + chunk])
            copy.start()
            copy.wait()

    @pl.loop(0, 6)
    def _(slot):
        for m in range(3):
            for copy in copies(slot, m):
                copy.wait_send()
        for face in range(2):

            def wait_outer():
                for copy in y_copies(slot, face, odds[0]):
                    copy.wait_send()

            for copy in y_copies(slot, face, 1 - odds[0]):
                copy.wait_send()
            for_outer(face, wait_outer)
        for copy in forward_copies(slot, 0):
            copy.wait_send()

    @pl.loop(0, 3)
    def _(chunk):
        @pl.when(chunk < 2)
        def _():
            for m in range(3):
                band_copy(chunk, m, 1 - band).wait_send()

            @pl.when(band == 0)
            def _():
                for copy in hops(0, chunk) + hops(2, chunk):
                    copy.wait_send()

        @pl.when((band == 0) & (chunk == 2))
        def _():
            for m in range(3):
                band_copy(2, m, 0).wait_send()

        pltpu.make_async_copy(fil.at[chunk], f_hbm.at[chunk], out_sem.at[chunk]).wait()


def filter_call(lines, pot):
    wh, wl = yz_weights()
    sel = face_weights()
    any_space = pl.BlockSpec(memory_space=pl.ANY)
    chunk = (3, CX, 8, CYZ)
    vm = pltpu.VMEM
    return pl.pallas_call(
        filter_kernel,
        out_shape=(
            jax.ShapeDtypeStruct(chunk, F32),
            jax.ShapeDtypeStruct(chunk, F32),
            jax.ShapeDtypeStruct((24, 128), F32),
        ),
        in_specs=[any_space] * 5,
        out_specs=(any_space, any_space, pl.BlockSpec(memory_space=pltpu.VMEM)),
        scratch_shapes=[
            vm((24 * 216, 128), F32),
            vm((216, 128), F32),
            vm(wh.shape, BF),
            vm(wl.shape, BF),
            vm(sel.shape, BF),
            vm((6, CX, 8, LANES), F32),
            vm((6, 2, 6, 8, CYZ), F32),
            vm((6, 9, 8, 384), F32),
            vm((6, 9, 8, 384), F32),
            vm((6, 9, 8, 384), F32),
            vm((6, 9, 8, 384), F32),
            vm((6, 2, 2, 8, 128), F32),
            vm((6, 2, 2, 8, 128), F32),
            vm((6, 2, 2, 8, 128), F32),
            vm((6, 2, 2, 8, 128), F32),
            vm((6, 2, 8, 128), F32),
            vm((6, 96, LANES), BF),
            vm((6, 96, LANES), BF),
            vm((96, 768), F32),
            vm(chunk, F32),
            vm(chunk, F32),
            vm((2, 6, 8, CYZ), F32),
            vm((2, 24, 128), F32),
            vm((22, 24, 128), F32),
            pltpu.SemaphoreType.DMA((7,)),
            pltpu.SemaphoreType.DMA((6,)),
            pltpu.SemaphoreType.DMA((6, 3, 6)),
            pltpu.SemaphoreType.DMA((6, 3, 6)),
            pltpu.SemaphoreType.DMA((6, 2, 2, 2)),
            pltpu.SemaphoreType.DMA((6, 2, 2, 2)),
            pltpu.SemaphoreType.DMA((6, 2)),
            pltpu.SemaphoreType.DMA((3, 2, 3)),
            pltpu.SemaphoreType.DMA((3, 2, 3)),
            pltpu.SemaphoreType.DMA((3, 3, 2)),
            pltpu.SemaphoreType.DMA((3, 3, 2)),
            pltpu.SemaphoreType.DMA((22,)),
            pltpu.SemaphoreType.DMA((22,)),
        ],
        compiler_params=pltpu.CompilerParams(collective_id=0, has_side_effects=True, vmem_limit_bytes=56 << 20),
        name="filter",
    )(lines, pot, jnp.asarray(wh), jnp.asarray(wl), jnp.asarray(sel))


def rotate_kernel(low, high, gram, out, mine, theirs, inverse, lines, sems, out_sems):
    band = lax.axis_index("band")

    def loads(x):
        own_load = pltpu.make_async_copy(low.at[:, x], mine.at[:, x], sems.at[0, x])
        return own_load, pltpu.make_async_copy(high.at[:, x], theirs.at[:, x], sems.at[1, x])

    for x in range(CX):
        loads(x)[0].start()

        @pl.when(band == 1)
        def _():
            loads(x)[1].start()

    g = gram[...] * (1.0 / (64 * CX * CYZ))
    blank = jnp.zeros((24, 16), F32)
    row, col = (lax.broadcasted_iota(jnp.int32, (48, 64), d) for d in range(2))
    left = jnp.concatenate(
        [jnp.concatenate([g[:, 0:24], g[:, 96:120], blank], 1), jnp.concatenate([g[:, 64:88], g[:, 32:56], blank], 1)], 0
    )
    table = jnp.concatenate([left, (row == col).astype(F32)], 1)
    rows = lax.broadcasted_iota(jnp.int32, (48, 128), 0)
    for k in range(0, 48, 2):
        one = jnp.broadcast_to(table[:, k : k + 1], (48, 128))
        two = jnp.broadcast_to(table[:, k + 1 : k + 2], (48, 128))
        a, b, c = one[k : k + 1], one[k + 1 : k + 2], two[k + 1 : k + 2]
        upper, lower = table[k : k + 1], table[k + 1 : k + 2]
        inverse[k : k + 1, :] = upper * lax.rsqrt(a)
        ratio = b / a
        inverse[k + 1 : k + 2, :] = (lower - ratio * upper) * lax.rsqrt(c - ratio * b)
        if k < 46:
            scale = 1.0 / (a * c - b * b)
            below = rows > k + 1
            table = (
                table
                - jnp.where(below, one, 0.0) * ((c * upper - b * lower) * scale)
                - jnp.where(below, two, 0.0) * ((a * lower - b * upper) * scale)
            )

    def sent(quarter):
        at = pl.ds(72 * quarter, 72)
        return pltpu.make_async_copy(lines.reshape(24, 216, 128).at[:, at], out.at[:, at], out_sems.at[quarter])

    def rotate(matrix, sources):
        mh, ml = split(matrix)
        left = jnp.concatenate([mh, ml, mh], 1)
        for x in range(CX):
            for load in loads(x)[: len(sources)]:
                load.wait()
            v = [source[:, x].reshape(24, CYZ) for source in sources]
            vh, vl = split(jnp.concatenate(v, 0) if len(v) > 1 else v[0])
            made = dot(left, jnp.concatenate([vh, vh, vl], 0))
            for t in range(18):
                lines[pl.ds(18 * x + t, 24, stride=216), :] = made[:, 128 * t : 128 * t + 128]
            if x % 4 == 3:
                sent(x // 4).start()

    @pl.when(band == 0)
    def _():
        rotate(inverse[0:24, 64:88], [mine])

    @pl.when(band == 1)
    def _():
        rotate(jnp.concatenate([inverse[24:48, 88:112], inverse[24:48, 64:88]], 1), [mine, theirs])

    for quarter in range(3):
        sent(quarter).wait()


def rotate_call(mine, theirs, gram):
    any_space = pl.BlockSpec(memory_space=pl.ANY)
    vm = pltpu.VMEM
    return pl.pallas_call(
        rotate_kernel,
        out_shape=jax.ShapeDtypeStruct((24, 216, 128), F32),
        in_specs=[any_space, any_space, pl.BlockSpec(memory_space=pltpu.VMEM)],
        out_specs=any_space,
        scratch_shapes=[
            vm((3, CX, 8, CYZ), F32),
            vm((3, CX, 8, CYZ), F32),
            vm((48, 128), F32),
            vm((24 * 216, 128), F32),
            pltpu.SemaphoreType.DMA((2, CX)),
            pltpu.SemaphoreType.DMA((3,)),
        ],
        compiler_params=pltpu.CompilerParams(vmem_limit_bytes=56 << 20),
        name="rotate",
    )(mine, theirs, gram)


def body(orbitals, potential):
    mine, theirs, gram = filter_call(orbitals.reshape(24 * 216, 128), potential.reshape(216, 128))
    return rotate_call(mine, theirs, gram).reshape(orbitals.shape)


def solution(mesh):
    return jax.shard_map(
        body,
        mesh=mesh,
        in_specs=(P("band", "dom", None, None), P("dom", None, None)),
        out_specs=P("band", "dom", None, None),
        check_vma=False,
    )
```

```python
import jax
import jax.numpy as jnp
import numpy as np
from jax import lax
from jax.experimental import pallas as pl
from jax.experimental.pallas import tpu as pltpu
from jax.sharding import PartitionSpec as P

CX = 12
CY = 48
CZ = 48
CYZ = CY * CZ
LANES = 3 * 128 + CYZ + 3 * 128
MESH = pl.DeviceIdType.MESH
BF = jnp.bfloat16
F32 = jnp.float32

stencil_weights = (
    -5369.0 / 1800.0,
    12.0 / 7.0,
    -15.0 / 56.0,
    10.0 / 189.0,
    -1.0 / 112.0,
    2.0 / 1925.0,
    -1.0 / 16632.0,
)
centre_shift = 7.25
half_width = 5.25
near = [-0.5 * w / half_width for w in stencil_weights]
own = (-1.5 * stencil_weights[0] - centre_shift) / half_width


def split_np(a):
    a = a.astype(np.float32)
    high = a.astype(BF)
    return high, (a - high.astype(np.float32)).astype(BF)


def yz_weights():
    out = np.zeros((3, 1280, 256), np.float64)
    for part in range(3):
        for n in range(256):
            cell = 256 * part + n
            row, z = cell // CZ, cell % CZ
            for k in range(1, 7):
                for sign in (-1, 1):
                    out[part, n + 384 + sign * CZ * k, n] += near[k]
                    at = z + sign * k
                    if 0 <= at < CZ:
                        out[part, n + 384 + sign * k, n] += near[k]
                    elif at < 0:
                        out[part, 1024 + row * 6 + at + 6, n] += near[k]
                    else:
                        out[part, 1152 + row * 6 + at - CZ, n] += near[k]
    return split_np(out)


def face_weights():
    out = np.zeros((768, 256), np.float32)
    for row in range(16):
        for i in range(6):
            out[row * CZ + i, row * 6 + i] = 1
            out[row * CZ + CZ - 6 + i, 128 + row * 6 + i] = 1
    return out.astype(BF)


def split(v):
    high = v.astype(BF)
    return high, (v - high.astype(F32)).astype(BF)


def dot(a, b):
    return jnp.dot(a, b, preferred_element_type=F32)


def dot_t(a, b):
    return lax.dot_general(a, b, (((1,), (1,)), ((), ())), preferred_element_type=F32)


def flipped(index, bit):
    return index + bit * (1 - 2 * (index // bit % 2))


def filter_kernel(
    orb, pot_hbm, wh_hbm, wl_hbm, sel_hbm, f_hbm, fo_hbm, gram,
    lin, pot, wh, wl, sel, cen, xrim, zlo, zhi, zlo_out, zhi_out, ylo, yhi, ylo_out, yhi_out, passed, vh, vl, yz, fil, oth, part, got,
    in_sem, out_sem, send_sem, recv_sem, y_send, y_recv, pass_send, band_send, band_recv, sum_send, sum_recv,
):
    band, dom = lax.axis_index("band"), lax.axis_index("dom")
    pairs = [(orb.at[pl.ds(1728 * c, 1728)], lin.at[pl.ds(1728 * c, 1728)]) for c in range(3)]
    pairs = pairs[:1] + [(sel_hbm, sel), (pot_hbm, pot), (wh_hbm, wh), (wl_hbm, wl)] + pairs[1:]
    loads = [pltpu.make_async_copy(a, b, in_sem.at[i]) for i, (a, b) in enumerate(pairs)]
    for load in loads:
        load.start()

    def across(z, core, y, x, other):
        to = dom
        for bit, used in enumerate((core, z % 2, z // 2, y % 2, y // 2, x)):
            if used:
                to = flipped(to, 1 << bit)
        return (1 - band if other else band), to

    stages = [
        [across(k // 2, k % 2, 0, 0, 0) for k in range(1, 8)],
        [across(0, 0, k // 4, k // 2 % 2, k % 2) for k in range(1, 16)],
    ]
    partners = [partner for stage in stages for partner in stage]
    barrier = pltpu.get_barrier_semaphore()
    for partner in partners:
        pl.semaphore_signal(barrier, 1, device_id=partner, device_id_type=MESH)

    ends, odds = [], []
    for first in (1, 4, 16):
        odd = (dom // first % 4 + 1) // 2 % 2
        below = odd * flipped(dom, first) + (1 - odd) * flipped(dom, 2 * first)
        above = odd * flipped(dom, 2 * first) + (1 - odd) * flipped(dom, first)
        ends.append(((band, below), (band, above)))
        odds.append(odd)

    def copies(slot, m):
        face = pl.ds(128 * m, 128)
        table = []
        for part in range(2):
            start = 768 * m + 384 * (part * odds[1] + (1 - part) * (1 - odds[1]))
            lanes, centre = pl.ds(start, 384), pl.ds(384 + start, 384)
            table += [
                (cen.at[slot, pl.ds(0, 6), :, centre], xrim.at[slot, 1, :, :, lanes], ends[0][0]),
                (cen.at[slot, pl.ds(6, 6), :, centre], xrim.at[slot, 0, :, :, lanes], ends[0][1]),
            ]
        table += [
            (zlo_out.at[slot, :, :, face], zhi.at[slot, :, :, face], ends[2][0]),
            (zhi_out.at[slot, :, :, face], zlo.at[slot, :, :, face], ends[2][1]),
        ]
        return [
            pltpu.make_async_remote_copy(
                a, b, send_sem.at[slot, m, i], recv_sem.at[slot, m, i], device_id=to, device_id_type=MESH
            )
            for i, (a, b, to) in enumerate(table)
        ]

    def y_moves(slot, face, half, sources, sems, to):
        rim = cen.at[slot, pl.ds(6 * half, 6), :, pl.ds((384 + CYZ, 128)[face], 256)]
        return [
            pltpu.make_async_remote_copy(
                a, b, sems[i], y_recv.at[slot, face, half, i], device_id=to, device_id_type=MESH
            )
            for i, (a, b) in enumerate(zip(sources, (rim, (yhi, ylo)[face].at[slot, half])))
        ]

    def y_copies(slot, face, half):
        sources = (
            cen.at[slot, pl.ds(6 * half, 6), :, pl.ds((384, 128 + CYZ)[face], 256)],
            (ylo_out, yhi_out)[face].at[slot, half],
        )
        sems = [y_send.at[slot, face, half, i] for i in range(2)]
        return y_moves(slot, face, half, sources, sems, ends[1][face])

    def forward_copies(slot, face):
        sources = (xrim.at[slot, odds[0], :, :, pl.ds((0, CYZ - 256)[face], 256)], passed.at[slot])
        sems = [pass_send.at[slot, i] for i in range(2)]
        return y_moves(slot, face, 1 - odds[0], sources, sems, (band, flipped(flipped(dom, 2), 4)))

    def band_copy(chunk, m, half):
        part_of = (chunk, pl.ds(6 * half, 6), slice(None), pl.ds(768 * m, 768))
        return pltpu.make_async_remote_copy(
            fil.at[part_of], oth.at[part_of], band_send.at[chunk, m, half], band_recv.at[chunk, m, half],
            device_id=(1 - band, dom), device_id_type=MESH,
        )

    lane = lax.broadcasted_iota(jnp.int32, (8, 128), 1)

    def group(i):
        return 2 - i + odds[1] * (2 * i - 2)

    def packed(tiles, shift):
        v = [pltpu.roll(tile, (32 * (q % 4) + shift) % 128, 1) for q, tile in enumerate(tiles)]
        first = jnp.where(lane < 64, jnp.where(lane < 32, v[0], v[1]), jnp.where(lane < 96, v[2], v[3]))
        return first, jnp.where(lane < 32, v[4], v[5])

    def for_outer(face, act):
        @pl.when(odds[1] == face)
        def _():
            act()

    def send_y(slot, face):
        start, shift = ((640, 0), (CYZ, 32))[face]
        for half in range(2):
            tiles = [cen[slot, 6 * half + q, :, pl.ds(start, 128)] for q in range(6)]
            out = (ylo_out, yhi_out)[face]
            out[slot, half, 0], out[slot, half, 1] = packed(tiles, shift)

        def start_outer():
            for copy in y_copies(slot, face, odds[0]):
                copy.start()

        for copy in y_copies(slot, face, 1 - odds[0]):
            copy.start()
        for_outer(face, start_outer)

    def forward(slot):
        for face in range(2):

            @pl.when(odds[1] == 1 - face)
            def _():
                start, shift = ((256, 0), (CYZ - 384, 32))[face]
                tiles = [xrim[slot, odds[0], q, :, pl.ds(start, 128)] for q in range(6)]
                passed[slot, 0], passed[slot, 1] = packed(tiles, shift)
                for copy in forward_copies(slot, face):
                    copy.start()

    def prepare(slot, m):
        lanes = pl.ds(pl.multiple_of(384 + 768 * m, 128), 768)
        face = pl.ds(pl.multiple_of(128 * m, 128), 128)
        high, low = split(cen[slot, :, :, lanes].reshape(96, 768))
        vh[slot, :, lanes] = high
        vl[slot, :, lanes] = low
        faces = dot(high, sel[...]) + dot(low, sel[...])
        for out, at in ((zlo_out, 0), (zhi_out, 128)):
            f = faces[:, at : at + 128].reshape(CX, 8, 128)
            for x in range(9):
                last = pltpu.roll(f[x // 3 * 4 + 3], 96 - 32 * (x % 3), 1)
                out[slot, x, :, face] = jnp.where(lane < 96, f[x // 3 * 4 + x % 3], last)

    def send(slot, m, first, count):
        for copy in copies(slot, m)[first : first + count]:
            copy.start()

    def split_rim(slot, face, rim, start, at, shift):
        for half in range(2):
            for copy in y_copies(slot, face, half):
                copy.wait_recv()
        for x in range(CX):
            tile = rim[slot, x // 6, x % 6 // 4]
            cen[slot, x, :, pl.ds(at, 128)] = pltpu.roll(tile, (shift - 32 * (x % 6 % 4)) % 128, 1)
        high, low = split(cen[slot, :, :, pl.ds(start, 384)].reshape(96, 384))
        vh[slot, :, pl.ds(start, 384)] = high
        vl[slot, :, pl.ds(start, 384)] = low

    def receive_y(slot, m):
        @pl.when(m == 0)
        def _():
            split_rim(slot, 1, ylo, 0, 0, 96)

        @pl.when(m == 2)
        def _():
            split_rim(slot, 0, yhi, 384 + CYZ, 640 + CYZ, 0)

    def receive(slot, m, first, count):
        for copy in copies(slot, m)[first : first + count]:
            copy.wait_recv()

    def arrive(slot, m, i, meanwhile):
        @pl.when(i == 0)
        def _():
            receive(slot, m, 0, 2)
            forward(slot)

        receive_y(slot, m)
        yz_product(slot, m)
        meanwhile()

        @pl.when(i > 0)
        def _():
            receive(slot, m, 0, 2)

        receive(slot, m, 2, 4)

    def z_rim(rim, slot, face):
        out = []
        for g in range(3):
            v = [rim[slot, 3 * g + q, :, face] for q in range(3)]
            r = [pltpu.roll(v[q], 32 + 32 * q, 1) for q in range(3)]
            out += v + [jnp.where(lane < 32, r[0], jnp.where(lane < 64, r[1], r[2]))]
        return jnp.concatenate(out, 0)

    def yz_product(slot, m):
        for j in range(3):
            window = pl.ds(pl.multiple_of(256 * j + 768 * m, 256), 1024)
            high, low = vh[slot, :, window], vl[slot, :, window]
            wide = dot(high, wh[j, 0:1024]) + dot(low, wh[j, 0:1024]) + dot(high, wl[j, 0:1024])
            yz[:, pl.ds(256 * j, 256)] = wide

    def rim_product(slot, m):
        face = pl.ds(pl.multiple_of(128 * m, 128), 128)
        high, low = split(jnp.concatenate([z_rim(zlo, slot, face), z_rim(zhi, slot, face)], 1))
        for j in range(3):
            rims = slice(1024, 1280)
            yz[:, pl.ds(256 * j, 256)] += dot(high, wh[j, rims]) + dot(low, wh[j, rims]) + dot(high, wl[j, rims])

    def stencil(slot, m, write):
        @pl.loop(0, 6)
        def _(t):
            at = pl.multiple_of(768 * m + 128 * t, 128)
            here, mid = pl.ds(at, 128), pl.ds(pl.multiple_of(at + 384, 128), 128)
            v = [xrim[slot, 0, i, :, here] for i in range(6)]
            v += [cen[slot, i, :, mid] for i in range(CX)]
            v += [xrim[slot, 1, i, :, here] for i in range(6)]
            for x in range(CX):
                diagonal = pot[pl.ds(18 * x + 6 * m + t, 1), :] * (1.0 / half_width) + own
                total = diagonal * v[x + 6] + yz[pl.ds(8 * x, 8), pl.ds(pl.multiple_of(128 * t, 128), 128)]
                for k in range(1, 7):
                    total = total + near[k] * (v[x + 6 - k] + v[x + 6 + k])
                write(x, here, mid, total)

    def relayout(chunk, m):
        for x in range(CX):
            for t in range(6):
                row = 8 * 216 * chunk + 18 * x + 6 * m + t
                lanes = pl.ds(pl.multiple_of(384 + 768 * m + 128 * t, 128), 128)
                cen[chunk, x, :, lanes] = lin[pl.ds(row, 8, stride=216), :]

    def rows(ref, m, first, layers):
        lanes = pl.ds(pl.multiple_of(768 * m, 128), 768)
        pieces = [split(ref[:, first + x, :, lanes].reshape(24, 768)) for x in range(layers)]
        return jnp.concatenate([jnp.concatenate([p[i] for p in pieces], 1) for i in range(2)], 0)

    def folded(a, b):
        products = dot_t(a, b)
        return products[:24, :24] + products[24:, :24] + products[:24, 24:]

    def own_products(m):
        a = rows(fil, m, 0, CX)
        part[0, :, 0:24] += folded(a, a)

    def enter(chunk):
        @pl.loop(0, 3)
        def _(i):
            relayout(chunk, group(i))

        if chunk > 0:

            @pl.loop(0, 3)
            def _(i):
                prepare(chunk, group(i))
                send(chunk, group(i), 4, 2)

    part[0] = jnp.zeros((24, 128), F32)
    loads[0].wait()
    loads[1].wait()
    enter(0)
    pl.semaphore_wait(barrier, len(partners))
    send(0, group(0), 0, 4)
    send_y(0, 0)
    send_y(0, 1)

    @pl.loop(0, 3)
    def _(i):
        @pl.when(i > 0)
        def _():
            send(0, group(i), 0, 4)

        prepare(0, group(i))
        send(0, group(i), 4, 2)

    for load in loads[2:]:
        load.wait()
    enter(1)

    @pl.loop(0, 3)
    def _(chunk):
        @pl.loop(0, 3)
        def _(i):
            m, slot = group(i), chunk

            def meanwhile():
                @pl.when((band == 0) & (chunk > 0))
                def _():
                    band_copy(chunk - 1, m, 0).start()

            arrive(slot, m, i, meanwhile)
            rim_product(slot, m)

            def write(x, here, mid, total):
                cen[chunk + 3, x, :, mid] = total

            stencil(slot, m, write)

            send(slot + 3, m, 0, 4)

            @pl.when(m == 0)
            def _():
                send_y(slot + 3, 0)

            @pl.when(m == 2)
            def _():
                send_y(slot + 3, 1)

            prepare(slot + 3, m)
            send(slot + 3, m, 4, 2)

        @pl.when(chunk == 0)
        def _():
            enter(2)

        @pl.when(chunk < 2)
        def _():
            send_y(chunk + 1, 0)
            send_y(chunk + 1, 1)

        @pl.loop(0, 3)
        def _(i):
            m, slot = group(i), chunk + 3
            arrive(slot, m, i, lambda: None)

            @pl.when(chunk < 2)
            def _():
                send(chunk + 1, m, 0, 4)

            rim_product(slot, m)

            def write(x, here, mid, total):
                fil[chunk, x, :, here] = 2.0 * total - cen[chunk, x, :, mid]

            stencil(slot, m, write)
            band_copy(chunk, m, 1 - band).start()

            @pl.when(chunk == 2)
            def _():
                own_products(m)

        pltpu.make_async_copy(fil.at[chunk], f_hbm.at[chunk], out_sem.at[chunk]).start()

    part[0] = jnp.where(band == 0, part[0], pltpu.roll(part[0], 32, 1))

    def cross_products(m):
        for chunk in range(3):
            band_copy(chunk, m, band).wait_recv()
        mine, theirs = rows(fil, m, 6 * band, 6), rows(oth, m, 6 * band, 6)
        first, second = jnp.where(band == 0, mine, theirs), jnp.where(band == 0, theirs, mine)
        part[0, :, 64:88] += folded(second, first)
        part[0, :, 96:120] += folded(first, second)

    @pl.loop(0, 3)
    def _(i):
        @pl.when(i == 2)
        def _():
            for m in range(3):
                band_copy(2, m, 1 - band).wait_send()

            @pl.when(band == 0)
            def _():
                for m in range(3):
                    band_copy(2, m, 0).start()

        cross_products(group(i))

    index = 0
    for number, stage in enumerate(stages):
        moves = []
        for partner in stage:
            moves.append(
                pltpu.make_async_remote_copy(
                    part.at[number], got.at[index], sum_send.at[index], sum_recv.at[index],
                    device_id=partner, device_id_type=MESH,
                )
            )
            moves[-1].start()
            index += 1
        for move in moves:
            move.wait_recv()
        terms = [part[number]] + [got[index - len(stage) + k] for k in range(len(stage))]
        while len(terms) > 1:
            terms = [a + b for a, b in zip(terms[::2], terms[1::2])]
        if number < 1:
            part[number + 1] = terms[0]
        else:
            gram[...] = terms[0]
        for move in moves:
            move.wait_send()

    @pl.when(band == 1)
    def _():
        @pl.loop(0, 3)
        def _(chunk):
            for m in range(3):
                band_copy(chunk, m, 0).wait_recv()
            copy = pltpu.make_async_copy(oth.at[chunk], fo_hbm.at[chunk], out_sem.at[3 + chunk])
            copy.start()
            copy.wait()

    @pl.loop(0, 6)
    def _(slot):
        for m in range(3):
            for copy in copies(slot, m):
                copy.wait_send()
        for face in range(2):

            def wait_outer():
                for copy in y_copies(slot, face, odds[0]):
                    copy.wait_send()

            for copy in y_copies(slot, face, 1 - odds[0]):
                copy.wait_send()
            for_outer(face, wait_outer)
        for copy in forward_copies(slot, 0):
            copy.wait_send()

    @pl.loop(0, 3)
    def _(chunk):
        @pl.when(chunk < 2)
        def _():
            for m in range(3):
                band_copy(chunk, m, 1 - band).wait_send()

        @pl.when(band == 0)
        def _():
            for m in range(3):
                band_copy(chunk, m, 0).wait_send()

        pltpu.make_async_copy(fil.at[chunk], f_hbm.at[chunk], out_sem.at[chunk]).wait()


def filter_call(lines, pot):
    wh, wl = yz_weights()
    sel = face_weights()
    any_space = pl.BlockSpec(memory_space=pl.ANY)
    chunk = (3, CX, 8, CYZ)
    vm = pltpu.VMEM
    return pl.pallas_call(
        filter_kernel,
        out_shape=(
            jax.ShapeDtypeStruct(chunk, F32),
            jax.ShapeDtypeStruct(chunk, F32),
            jax.ShapeDtypeStruct((24, 128), F32),
        ),
        in_specs=[any_space] * 5,
        out_specs=(any_space, any_space, pl.BlockSpec(memory_space=pltpu.VMEM)),
        scratch_shapes=[
            vm((24 * 216, 128), F32),
            vm((216, 128), F32),
            vm(wh.shape, BF),
            vm(wl.shape, BF),
            vm(sel.shape, BF),
            vm((6, CX, 8, LANES), F32),
            vm((6, 2, 6, 8, CYZ), F32),
            vm((6, 9, 8, 384), F32),
            vm((6, 9, 8, 384), F32),
            vm((6, 9, 8, 384), F32),
            vm((6, 9, 8, 384), F32),
            vm((6, 2, 2, 8, 128), F32),
            vm((6, 2, 2, 8, 128), F32),
            vm((6, 2, 2, 8, 128), F32),
            vm((6, 2, 2, 8, 128), F32),
            vm((6, 2, 8, 128), F32),
            vm((6, 96, LANES), BF),
            vm((6, 96, LANES), BF),
            vm((96, 768), F32),
            vm(chunk, F32),
            vm(chunk, F32),
            vm((2, 24, 128), F32),
            vm((22, 24, 128), F32),
            pltpu.SemaphoreType.DMA((7,)),
            pltpu.SemaphoreType.DMA((6,)),
            pltpu.SemaphoreType.DMA((6, 3, 6)),
            pltpu.SemaphoreType.DMA((6, 3, 6)),
            pltpu.SemaphoreType.DMA((6, 2, 2, 2)),
            pltpu.SemaphoreType.DMA((6, 2, 2, 2)),
            pltpu.SemaphoreType.DMA((6, 2)),
            pltpu.SemaphoreType.DMA((3, 3, 2)),
            pltpu.SemaphoreType.DMA((3, 3, 2)),
            pltpu.SemaphoreType.DMA((22,)),
            pltpu.SemaphoreType.DMA((22,)),
        ],
        compiler_params=pltpu.CompilerParams(collective_id=0, has_side_effects=True, vmem_limit_bytes=56 << 20),
        name="filter",
    )(lines, pot, jnp.asarray(wh), jnp.asarray(wl), jnp.asarray(sel))


def rotate_kernel(low, high, gram, out, mine, theirs, inverse, lines, sems, out_sems):
    band = lax.axis_index("band")

    def loads(x):
        own_load = pltpu.make_async_copy(low.at[:, x], mine.at[:, x], sems.at[0, x])
        return own_load, pltpu.make_async_copy(high.at[:, x], theirs.at[:, x], sems.at[1, x])

    for x in range(CX):
        loads(x)[0].start()

        @pl.when(band == 1)
        def _():
            loads(x)[1].start()

    g = gram[...] * (1.0 / (64 * CX * CYZ))
    blank = jnp.zeros((24, 16), F32)
    row, col = (lax.broadcasted_iota(jnp.int32, (48, 64), d) for d in range(2))
    left = jnp.concatenate(
        [jnp.concatenate([g[:, 0:24], g[:, 96:120], blank], 1), jnp.concatenate([g[:, 64:88], g[:, 32:56], blank], 1)], 0
    )
    table = jnp.concatenate([left, (row == col).astype(F32)], 1)
    rows = lax.broadcasted_iota(jnp.int32, (48, 128), 0)
    for k in range(0, 48, 2):
        one = jnp.broadcast_to(table[:, k : k + 1], (48, 128))
        two = jnp.broadcast_to(table[:, k + 1 : k + 2], (48, 128))
        a, b, c = one[k : k + 1], one[k + 1 : k + 2], two[k + 1 : k + 2]
        upper, lower = table[k : k + 1], table[k + 1 : k + 2]
        inverse[k : k + 1, :] = upper * lax.rsqrt(a)
        ratio = b / a
        inverse[k + 1 : k + 2, :] = (lower - ratio * upper) * lax.rsqrt(c - ratio * b)
        if k < 46:
            scale = 1.0 / (a * c - b * b)
            below = rows > k + 1
            table = (
                table
                - jnp.where(below, one, 0.0) * ((c * upper - b * lower) * scale)
                - jnp.where(below, two, 0.0) * ((a * lower - b * upper) * scale)
            )

    def sent(quarter):
        at = pl.ds(72 * quarter, 72)
        return pltpu.make_async_copy(lines.reshape(24, 216, 128).at[:, at], out.at[:, at], out_sems.at[quarter])

    def rotate(matrix, sources):
        mh, ml = split(matrix)
        left = jnp.concatenate([jnp.concatenate([mh, mh], 1), jnp.concatenate([ml, jnp.zeros_like(ml)], 1)], 0)
        for x in range(CX):
            for load in loads(x)[: len(sources)]:
                load.wait()
            v = [source[:, x].reshape(24, CYZ) for source in sources]
            vh, vl = split(jnp.concatenate(v, 0) if len(v) > 1 else v[0])
            made = dot(left, jnp.concatenate([vh, vl], 0))
            made = made[:24] + made[24:]
            for t in range(18):
                lines[pl.ds(18 * x + t, 24, stride=216), :] = made[:, 128 * t : 128 * t + 128]
            if x % 4 == 3:
                sent(x // 4).start()

    @pl.when(band == 0)
    def _():
        rotate(inverse[0:24, 64:88], [mine])

    @pl.when(band == 1)
    def _():
        rotate(jnp.concatenate([inverse[24:48, 88:112], inverse[24:48, 64:88]], 1), [mine, theirs])

    for quarter in range(3):
        sent(quarter).wait()


def rotate_call(mine, theirs, gram):
    any_space = pl.BlockSpec(memory_space=pl.ANY)
    vm = pltpu.VMEM
    return pl.pallas_call(
        rotate_kernel,
        out_shape=jax.ShapeDtypeStruct((24, 216, 128), F32),
        in_specs=[any_space, any_space, pl.BlockSpec(memory_space=pltpu.VMEM)],
        out_specs=any_space,
        scratch_shapes=[
            vm((3, CX, 8, CYZ), F32),
            vm((3, CX, 8, CYZ), F32),
            vm((48, 128), F32),
            vm((24 * 216, 128), F32),
            pltpu.SemaphoreType.DMA((2, CX)),
            pltpu.SemaphoreType.DMA((3,)),
        ],
        compiler_params=pltpu.CompilerParams(vmem_limit_bytes=56 << 20),
        name="rotate",
    )(mine, theirs, gram)


def body(orbitals, potential):
    mine, theirs, gram = filter_call(orbitals.reshape(24 * 216, 128), potential.reshape(216, 128))
    return rotate_call(mine, theirs, gram).reshape(orbitals.shape)


def solution(mesh):
    return jax.shard_map(
        body,
        mesh=mesh,
        in_specs=(P("band", "dom", None, None), P("dom", None, None)),
        out_specs=P("band", "dom", None, None),
        check_vma=False,
    )
```

```python
import jax
import jax.numpy as jnp
import numpy as np
from jax import lax
from jax.experimental import pallas as pl
from jax.experimental.pallas import tpu as pltpu
from jax.sharding import PartitionSpec as P

CX = 12
CY = 48
CZ = 48
CYZ = CY * CZ
LANES = 3 * 128 + CYZ + 3 * 128
MESH = pl.DeviceIdType.MESH
BF = jnp.bfloat16
F32 = jnp.float32

stencil_weights = (
    -5369.0 / 1800.0,
    12.0 / 7.0,
    -15.0 / 56.0,
    10.0 / 189.0,
    -1.0 / 112.0,
    2.0 / 1925.0,
    -1.0 / 16632.0,
)
centre_shift = 7.25
half_width = 5.25
near = [-0.5 * w / half_width for w in stencil_weights]
own = (-1.5 * stencil_weights[0] - centre_shift) / half_width


def split_np(a):
    a = a.astype(np.float32)
    high = a.astype(BF)
    return high, (a - high.astype(np.float32)).astype(BF)


def yz_weights():
    out = np.zeros((3, 1280, 256), np.float64)
    for part in range(3):
        for n in range(256):
            cell = 256 * part + n
            row, z = cell // CZ, cell % CZ
            for k in range(1, 7):
                for sign in (-1, 1):
                    out[part, n + 384 + sign * CZ * k, n] += near[k]
                    at = z + sign * k
                    if 0 <= at < CZ:
                        out[part, n + 384 + sign * k, n] += near[k]
                    elif at < 0:
                        out[part, 1024 + row * 6 + at + 6, n] += near[k]
                    else:
                        out[part, 1152 + row * 6 + at - CZ, n] += near[k]
    return split_np(out)


def face_weights():
    out = np.zeros((768, 256), np.float32)
    for row in range(16):
        for i in range(6):
            out[row * CZ + i, row * 6 + i] = 1
            out[row * CZ + CZ - 6 + i, 128 + row * 6 + i] = 1
    return out.astype(BF)


def split(v):
    high = v.astype(BF)
    return high, (v - high.astype(F32)).astype(BF)


def dot(a, b):
    return jnp.dot(a, b, preferred_element_type=F32)


def dot_t(a, b):
    return lax.dot_general(a, b, (((1,), (1,)), ((), ())), preferred_element_type=F32)


def flipped(index, bit):
    return index + bit * (1 - 2 * (index // bit % 2))


def filter_kernel(
    orb, pot_hbm, wh_hbm, wl_hbm, sel_hbm, f_hbm, fo_hbm, gram,
    lin, pot, wh, wl, sel, cen, xrim, zlo, zhi, zlo_out, zhi_out, ylo, yhi, ylo_out, yhi_out, passed, vh, vl, yz, fil, oth, acc, part, got,
    in_sem, out_sem, send_sem, recv_sem, y_send, y_recv, pass_send, band_send, band_recv, sum_send, sum_recv,
):
    band, dom = lax.axis_index("band"), lax.axis_index("dom")
    pairs = [(orb.at[pl.ds(1728 * c, 1728)], lin.at[pl.ds(1728 * c, 1728)]) for c in range(3)]
    pairs = pairs[:1] + [(sel_hbm, sel), (pot_hbm, pot), (wh_hbm, wh), (wl_hbm, wl)] + pairs[1:]
    loads = [pltpu.make_async_copy(a, b, in_sem.at[i]) for i, (a, b) in enumerate(pairs)]
    for load in loads:
        load.start()

    def across(z, core, y, x, other):
        to = dom
        for bit, used in enumerate((core, z % 2, z // 2, y % 2, y // 2, x)):
            if used:
                to = flipped(to, 1 << bit)
        return (1 - band if other else band), to

    stages = [
        [across(k // 2, k % 2, 0, 0, 0) for k in range(1, 8)],
        [across(0, 0, k // 4, k // 2 % 2, k % 2) for k in range(1, 16)],
    ]
    partners = [partner for stage in stages for partner in stage]
    barrier = pltpu.get_barrier_semaphore()
    for partner in partners:
        pl.semaphore_signal(barrier, 1, device_id=partner, device_id_type=MESH)

    ends, odds = [], []
    for first in (1, 4, 16):
        odd = (dom // first % 4 + 1) // 2 % 2
        below = odd * flipped(dom, first) + (1 - odd) * flipped(dom, 2 * first)
        above = odd * flipped(dom, 2 * first) + (1 - odd) * flipped(dom, first)
        ends.append(((band, below), (band, above)))
        odds.append(odd)

    def copies(slot, m):
        face = pl.ds(128 * m, 128)
        table = []
        for part in range(2):
            start = 768 * m + 384 * (part * odds[1] + (1 - part) * (1 - odds[1]))
            lanes, centre = pl.ds(start, 384), pl.ds(384 + start, 384)
            table += [
                (cen.at[slot, pl.ds(0, 6), :, centre], xrim.at[slot, 1, :, :, lanes], ends[0][0]),
                (cen.at[slot, pl.ds(6, 6), :, centre], xrim.at[slot, 0, :, :, lanes], ends[0][1]),
            ]
        table += [
            (zlo_out.at[slot, :, :, face], zhi.at[slot, :, :, face], ends[2][0]),
            (zhi_out.at[slot, :, :, face], zlo.at[slot, :, :, face], ends[2][1]),
        ]
        return [
            pltpu.make_async_remote_copy(
                a, b, send_sem.at[slot, m, i], recv_sem.at[slot, m, i], device_id=to, device_id_type=MESH
            )
            for i, (a, b, to) in enumerate(table)
        ]

    def y_moves(slot, face, half, sources, sems, to):
        rim = cen.at[slot, pl.ds(6 * half, 6), :, pl.ds((384 + CYZ, 128)[face], 256)]
        return [
            pltpu.make_async_remote_copy(
                a, b, sems[i], y_recv.at[slot, face, half, i], device_id=to, device_id_type=MESH
            )
            for i, (a, b) in enumerate(zip(sources, (rim, (yhi, ylo)[face].at[slot, half])))
        ]

    def y_copies(slot, face, half):
        sources = (
            cen.at[slot, pl.ds(6 * half, 6), :, pl.ds((384, 128 + CYZ)[face], 256)],
            (ylo_out, yhi_out)[face].at[slot, half],
        )
        sems = [y_send.at[slot, face, half, i] for i in range(2)]
        return y_moves(slot, face, half, sources, sems, ends[1][face])

    def forward_copies(slot, face):
        sources = (xrim.at[slot, odds[0], :, :, pl.ds((0, CYZ - 256)[face], 256)], passed.at[slot])
        sems = [pass_send.at[slot, i] for i in range(2)]
        return y_moves(slot, face, 1 - odds[0], sources, sems, (band, flipped(flipped(dom, 2), 4)))

    def band_copy(chunk, m, half):
        part_of = (chunk, pl.ds(6 * half, 6), slice(None), pl.ds(768 * m, 768))
        return pltpu.make_async_remote_copy(
            fil.at[part_of], oth.at[part_of], band_send.at[chunk, m, half], band_recv.at[chunk, m, half],
            device_id=(1 - band, dom), device_id_type=MESH,
        )

    lane = lax.broadcasted_iota(jnp.int32, (8, 128), 1)

    def group(i):
        return 2 - i + odds[1] * (2 * i - 2)

    def packed(tiles, shift):
        v = [pltpu.roll(tile, (32 * (q % 4) + shift) % 128, 1) for q, tile in enumerate(tiles)]
        first = jnp.where(lane < 64, jnp.where(lane < 32, v[0], v[1]), jnp.where(lane < 96, v[2], v[3]))
        return first, jnp.where(lane < 32, v[4], v[5])

    def for_outer(face, act):
        @pl.when(odds[1] == face)
        def _():
            act()

    def send_y(slot, face):
        start, shift = ((640, 0), (CYZ, 32))[face]
        for half in range(2):
            tiles = [cen[slot, 6 * half + q, :, pl.ds(start, 128)] for q in range(6)]
            out = (ylo_out, yhi_out)[face]
            out[slot, half, 0], out[slot, half, 1] = packed(tiles, shift)

        def start_outer():
            for copy in y_copies(slot, face, odds[0]):
                copy.start()

        for copy in y_copies(slot, face, 1 - odds[0]):
            copy.start()
        for_outer(face, start_outer)

    def forward(slot):
        for face in range(2):

            @pl.when(odds[1] == 1 - face)
            def _():
                start, shift = ((256, 0), (CYZ - 384, 32))[face]
                tiles = [xrim[slot, odds[0], q, :, pl.ds(start, 128)] for q in range(6)]
                passed[slot, 0], passed[slot, 1] = packed(tiles, shift)
                for copy in forward_copies(slot, face):
                    copy.start()

    def prepare(slot, m):
        lanes = pl.ds(pl.multiple_of(384 + 768 * m, 128), 768)
        face = pl.ds(pl.multiple_of(128 * m, 128), 128)
        high, low = split(cen[slot, :, :, lanes].reshape(96, 768))
        vh[slot, :, lanes] = high
        vl[slot, :, lanes] = low
        faces = dot(high, sel[...]) + dot(low, sel[...])
        for out, at in ((zlo_out, 0), (zhi_out, 128)):
            f = faces[:, at : at + 128].reshape(CX, 8, 128)
            for x in range(9):
                last = pltpu.roll(f[x // 3 * 4 + 3], 96 - 32 * (x % 3), 1)
                out[slot, x, :, face] = jnp.where(lane < 96, f[x // 3 * 4 + x % 3], last)

    def send(slot, m, first, count):
        for copy in copies(slot, m)[first : first + count]:
            copy.start()

    def split_rim(slot, face, rim, start, at, shift):
        for half in range(2):
            for copy in y_copies(slot, face, half):
                copy.wait_recv()
        for x in range(CX):
            tile = rim[slot, x // 6, x % 6 // 4]
            cen[slot, x, :, pl.ds(at, 128)] = pltpu.roll(tile, (shift - 32 * (x % 6 % 4)) % 128, 1)
        high, low = split(cen[slot, :, :, pl.ds(start, 384)].reshape(96, 384))
        vh[slot, :, pl.ds(start, 384)] = high
        vl[slot, :, pl.ds(start, 384)] = low

    def receive_y(slot, m):
        @pl.when(m == 0)
        def _():
            split_rim(slot, 1, ylo, 0, 0, 96)

        @pl.when(m == 2)
        def _():
            split_rim(slot, 0, yhi, 384 + CYZ, 640 + CYZ, 0)

    def receive(slot, m, first, count):
        for copy in copies(slot, m)[first : first + count]:
            copy.wait_recv()

    def arrive(slot, m, i, meanwhile):
        @pl.when(i == 0)
        def _():
            receive(slot, m, 0, 2)
            forward(slot)

        receive_y(slot, m)
        yz_product(slot, m)
        meanwhile()

        @pl.when(i > 0)
        def _():
            receive(slot, m, 0, 2)

        receive(slot, m, 2, 4)

    def z_rim(rim, slot, face):
        out = []
        for g in range(3):
            v = [rim[slot, 3 * g + q, :, face] for q in range(3)]
            r = [pltpu.roll(v[q], 32 + 32 * q, 1) for q in range(3)]
            out += v + [jnp.where(lane < 32, r[0], jnp.where(lane < 64, r[1], r[2]))]
        return jnp.concatenate(out, 0)

    def yz_product(slot, m):
        for j in range(3):
            window = pl.ds(pl.multiple_of(256 * j + 768 * m, 256), 1024)
            high, low = vh[slot, :, window], vl[slot, :, window]
            wide = dot(high, wh[j, 0:1024]) + dot(low, wh[j, 0:1024]) + dot(high, wl[j, 0:1024])
            yz[:, pl.ds(256 * j, 256)] = wide

    def rim_product(slot, m):
        face = pl.ds(pl.multiple_of(128 * m, 128), 128)
        high, low = split(jnp.concatenate([z_rim(zlo, slot, face), z_rim(zhi, slot, face)], 1))
        for j in range(3):
            rims = slice(1024, 1280)
            yz[:, pl.ds(256 * j, 256)] += dot(high, wh[j, rims]) + dot(low, wh[j, rims]) + dot(high, wl[j, rims])

    def stencil(slot, m, write):
        @pl.loop(0, 6)
        def _(t):
            at = pl.multiple_of(768 * m + 128 * t, 128)
            here, mid = pl.ds(at, 128), pl.ds(pl.multiple_of(at + 384, 128), 128)
            v = [xrim[slot, 0, i, :, here] for i in range(6)]
            v += [cen[slot, i, :, mid] for i in range(CX)]
            v += [xrim[slot, 1, i, :, here] for i in range(6)]
            for x in range(CX):
                diagonal = pot[pl.ds(18 * x + 6 * m + t, 1), :] * (1.0 / half_width) + own
                total = diagonal * v[x + 6] + yz[pl.ds(8 * x, 8), pl.ds(pl.multiple_of(128 * t, 128), 128)]
                for k in range(1, 7):
                    total = total + near[k] * (v[x + 6 - k] + v[x + 6 + k])
                write(x, here, mid, total)

    def relayout(chunk, m):
        for x in range(CX):
            for t in range(6):
                row = 8 * 216 * chunk + 18 * x + 6 * m + t
                lanes = pl.ds(pl.multiple_of(384 + 768 * m + 128 * t, 128), 128)
                cen[chunk, x, :, lanes] = lin[pl.ds(row, 8, stride=216), :]

    def rows(ref, m, first, layers):
        lanes = pl.ds(pl.multiple_of(768 * m, 128), 768)
        pieces = [split(ref[:, first + x, :, lanes].reshape(24, 768)) for x in range(layers)]
        return jnp.concatenate([jnp.concatenate([p[i] for p in pieces], 1) for i in range(2)], 0)

    def folded(a, b):
        products = dot_t(a, b)
        return products[:24, :24] + products[24:, :24] + products[:24, 24:]

    def own_products(m):
        a = rows(fil, m, 0, CX)
        acc[:, 0:24] += folded(a, a)

    def enter(chunk):
        @pl.loop(0, 3)
        def _(i):
            relayout(chunk, group(i))

        if chunk > 0:

            @pl.loop(0, 3)
            def _(i):
                prepare(chunk, group(i))
                send(chunk, group(i), 4, 2)

    acc[...] = jnp.zeros_like(acc)
    loads[0].wait()
    loads[1].wait()
    enter(0)
    pl.semaphore_wait(barrier, len(partners))
    send(0, group(0), 0, 4)
    send_y(0, 0)
    send_y(0, 1)

    @pl.loop(0, 3)
    def _(i):
        @pl.when(i > 0)
        def _():
            send(0, group(i), 0, 4)

        prepare(0, group(i))
        send(0, group(i), 4, 2)

    for load in loads[2:]:
        load.wait()
    enter(1)

    @pl.loop(0, 3)
    def _(chunk):
        @pl.loop(0, 3)
        def _(i):
            m, slot = group(i), chunk

            def meanwhile():
                @pl.when((band == 0) & (chunk > 0))
                def _():
                    band_copy(chunk - 1, m, 0).start()

            arrive(slot, m, i, meanwhile)
            rim_product(slot, m)

            def write(x, here, mid, total):
                cen[chunk + 3, x, :, mid] = total

            stencil(slot, m, write)

            send(slot + 3, m, 0, 4)

            @pl.when(m == 0)
            def _():
                send_y(slot + 3, 0)

            @pl.when(m == 2)
            def _():
                send_y(slot + 3, 1)

            prepare(slot + 3, m)
            send(slot + 3, m, 4, 2)

        @pl.when(chunk == 0)
        def _():
            enter(2)

        @pl.when(chunk < 2)
        def _():
            send_y(chunk + 1, 0)
            send_y(chunk + 1, 1)

        @pl.loop(0, 3)
        def _(i):
            m, slot = group(i), chunk + 3
            arrive(slot, m, i, lambda: None)

            @pl.when(chunk < 2)
            def _():
                send(chunk + 1, m, 0, 4)

            rim_product(slot, m)

            def write(x, here, mid, total):
                fil[chunk, x, :, here] = 2.0 * total - cen[chunk, x, :, mid]

            stencil(slot, m, write)
            band_copy(chunk, m, 1 - band).start()

            @pl.when(chunk == 2)
            def _():
                own_products(m)

        pltpu.make_async_copy(fil.at[chunk], f_hbm.at[chunk], out_sem.at[chunk]).start()

    def cross_products(m):
        for chunk in range(3):
            band_copy(chunk, m, band).wait_recv()
        mine, theirs = rows(fil, m, 6 * band, 6), rows(oth, m, 6 * band, 6)
        first, second = jnp.where(band == 0, mine, theirs), jnp.where(band == 0, theirs, mine)
        acc[:, 64:88] += folded(second, first)

    @pl.loop(0, 3)
    def _(i):
        @pl.when(i == 2)
        def _():
            for m in range(3):
                band_copy(2, m, 1 - band).wait_send()

            @pl.when(band == 0)
            def _():
                for m in range(3):
                    band_copy(2, m, 0).start()

        cross_products(group(i))

    v = acc[...]
    alone = jnp.where(lax.broadcasted_iota(jnp.int32, (24, 128), 1) < 24, v, 0.0)
    cross = v - alone
    tail = pltpu.roll(alone[16:], 72, 1)
    part[0] = (
        jnp.where(band == 0, alone[:16], pltpu.roll(alone[:16], 24, 1))
        + pltpu.roll(cross[:16], 112, 1)
        + jnp.concatenate([jnp.where(band == 0, tail, 0.0) + pltpu.roll(cross[16:], 32, 1), jnp.where(band == 0, 0.0, tail)], 0)
    )

    index = 0
    for number, stage in enumerate(stages):
        moves = []
        for partner in stage:
            moves.append(
                pltpu.make_async_remote_copy(
                    part.at[number], got.at[index], sum_send.at[index], sum_recv.at[index],
                    device_id=partner, device_id_type=MESH,
                )
            )
            index += 1
        for move in moves:
            move.start()
        for move in moves:
            move.wait_recv()
        terms = [part[number]] + [got[index - len(stage) + k] for k in range(len(stage))]
        while len(terms) > 1:
            terms = [a + b for a, b in zip(terms[::2], terms[1::2])]
        if number < 1:
            part[number + 1] = terms[0]
        else:
            gram[...] = terms[0]
        for move in moves:
            move.wait_send()

    @pl.when(band == 1)
    def _():
        @pl.loop(0, 3)
        def _(chunk):
            for m in range(3):
                band_copy(chunk, m, 0).wait_recv()
            copy = pltpu.make_async_copy(oth.at[chunk], fo_hbm.at[chunk], out_sem.at[3 + chunk])
            copy.start()
            copy.wait()

    @pl.loop(0, 6)
    def _(slot):
        for m in range(3):
            for copy in copies(slot, m):
                copy.wait_send()
        for face in range(2):

            def wait_outer():
                for copy in y_copies(slot, face, odds[0]):
                    copy.wait_send()

            for copy in y_copies(slot, face, 1 - odds[0]):
                copy.wait_send()
            for_outer(face, wait_outer)
        for copy in forward_copies(slot, 0):
            copy.wait_send()

    @pl.loop(0, 3)
    def _(chunk):
        @pl.when(chunk < 2)
        def _():
            for m in range(3):
                band_copy(chunk, m, 1 - band).wait_send()

        @pl.when(band == 0)
        def _():
            for m in range(3):
                band_copy(chunk, m, 0).wait_send()

        pltpu.make_async_copy(fil.at[chunk], f_hbm.at[chunk], out_sem.at[chunk]).wait()


def filter_call(lines, pot):
    wh, wl = yz_weights()
    sel = face_weights()
    any_space = pl.BlockSpec(memory_space=pl.ANY)
    chunk = (3, CX, 8, CYZ)
    vm = pltpu.VMEM
    return pl.pallas_call(
        filter_kernel,
        out_shape=(
            jax.ShapeDtypeStruct(chunk, F32),
            jax.ShapeDtypeStruct(chunk, F32),
            jax.ShapeDtypeStruct((16, 128), F32),
        ),
        in_specs=[any_space] * 5,
        out_specs=(any_space, any_space, pl.BlockSpec(memory_space=pltpu.VMEM)),
        scratch_shapes=[
            vm((24 * 216, 128), F32),
            vm((216, 128), F32),
            vm(wh.shape, BF),
            vm(wl.shape, BF),
            vm(sel.shape, BF),
            vm((6, CX, 8, LANES), F32),
            vm((6, 2, 6, 8, CYZ), F32),
            vm((6, 9, 8, 384), F32),
            vm((6, 9, 8, 384), F32),
            vm((6, 9, 8, 384), F32),
            vm((6, 9, 8, 384), F32),
            vm((6, 2, 2, 8, 128), F32),
            vm((6, 2, 2, 8, 128), F32),
            vm((6, 2, 2, 8, 128), F32),
            vm((6, 2, 2, 8, 128), F32),
            vm((6, 2, 8, 128), F32),
            vm((6, 96, LANES), BF),
            vm((6, 96, LANES), BF),
            vm((96, 768), F32),
            vm(chunk, F32),
            vm(chunk, F32),
            vm((24, 128), F32),
            vm((2, 16, 128), F32),
            vm((22, 16, 128), F32),
            pltpu.SemaphoreType.DMA((7,)),
            pltpu.SemaphoreType.DMA((6,)),
            pltpu.SemaphoreType.DMA((6, 3, 6)),
            pltpu.SemaphoreType.DMA((6, 3, 6)),
            pltpu.SemaphoreType.DMA((6, 2, 2, 2)),
            pltpu.SemaphoreType.DMA((6, 2, 2, 2)),
            pltpu.SemaphoreType.DMA((6, 2)),
            pltpu.SemaphoreType.DMA((3, 3, 2)),
            pltpu.SemaphoreType.DMA((3, 3, 2)),
            pltpu.SemaphoreType.DMA((22,)),
            pltpu.SemaphoreType.DMA((22,)),
        ],
        compiler_params=pltpu.CompilerParams(collective_id=0, has_side_effects=True, vmem_limit_bytes=56 << 20),
        name="filter",
    )(lines, pot, jnp.asarray(wh), jnp.asarray(wl), jnp.asarray(sel))


def rotate_kernel(low, high, gram, out, mine, theirs, inverse, lines, sems, out_sems):
    band = lax.axis_index("band")

    def loads(x):
        own_load = pltpu.make_async_copy(low.at[:, x], mine.at[:, x], sems.at[0, x])
        return own_load, pltpu.make_async_copy(high.at[:, x], theirs.at[:, x], sems.at[1, x])

    for x in range(CX):
        loads(x)[0].start()

        @pl.when(band == 1)
        def _():
            loads(x)[1].start()

    g = gram[...] * (1.0 / (64 * CX * CYZ))
    blank = jnp.zeros((24, 16), F32)
    row, col = (lax.broadcasted_iota(jnp.int32, (48, 64), d) for d in range(2))
    unit = (row == col).astype(F32)
    first = jnp.concatenate([g[:, 0:24], g[0:8, 72:96]], 0)
    second = jnp.concatenate([g[:, 24:48], g[8:16, 72:96]], 0)
    cross = jnp.concatenate([g[:, 48:72], g[0:8, 96:120]], 0)
    turned = lax.dot_general(unit[:24, :24], cross, (((1,), (1,)), ((), ())), precision=lax.Precision.HIGHEST)
    left = jnp.concatenate(
        [jnp.concatenate([first, turned, blank], 1), jnp.concatenate([cross, second, blank], 1)], 0
    )
    table = jnp.concatenate([left, unit], 1)
    rows = lax.broadcasted_iota(jnp.int32, (48, 128), 0)
    for k in range(0, 48, 2):
        one = jnp.broadcast_to(table[:, k : k + 1], (48, 128))
        two = jnp.broadcast_to(table[:, k + 1 : k + 2], (48, 128))
        a, b, c = one[k : k + 1], one[k + 1 : k + 2], two[k + 1 : k + 2]
        upper, lower = table[k : k + 1], table[k + 1 : k + 2]
        inverse[k : k + 1, :] = upper * lax.rsqrt(a)
        ratio = b / a
        inverse[k + 1 : k + 2, :] = (lower - ratio * upper) * lax.rsqrt(c - ratio * b)
        if k < 46:
            scale = 1.0 / (a * c - b * b)
            below = rows > k + 1
            table = (
                table
                - jnp.where(below, one, 0.0) * ((c * upper - b * lower) * scale)
                - jnp.where(below, two, 0.0) * ((a * lower - b * upper) * scale)
            )

    def sent(quarter):
        at = pl.ds(72 * quarter, 72)
        return pltpu.make_async_copy(lines.reshape(24, 216, 128).at[:, at], out.at[:, at], out_sems.at[quarter])

    def rotate(matrix, sources):
        mh, ml = split(matrix)
        left = jnp.concatenate([jnp.concatenate([mh, mh], 1), jnp.concatenate([ml, jnp.zeros_like(ml)], 1)], 0)
        for x in range(CX):
            for load in loads(x)[: len(sources)]:
                load.wait()
            v = [source[:, x].reshape(24, CYZ) for source in sources]
            vh, vl = split(jnp.concatenate(v, 0) if len(v) > 1 else v[0])
            made = dot(left, jnp.concatenate([vh, vl], 0))
            made = made[:24] + made[24:]
            for t in range(18):
                lines[pl.ds(18 * x + t, 24, stride=216), :] = made[:, 128 * t : 128 * t + 128]
            if x % 4 == 3:
                sent(x // 4).start()

    @pl.when(band == 0)
    def _():
        rotate(inverse[0:24, 64:88], [mine])

    @pl.when(band == 1)
    def _():
        rotate(jnp.concatenate([inverse[24:48, 88:112], inverse[24:48, 64:88]], 1), [mine, theirs])

    for quarter in range(3):
        sent(quarter).wait()


def rotate_call(mine, theirs, gram):
    any_space = pl.BlockSpec(memory_space=pl.ANY)
    vm = pltpu.VMEM
    return pl.pallas_call(
        rotate_kernel,
        out_shape=jax.ShapeDtypeStruct((24, 216, 128), F32),
        in_specs=[any_space, any_space, pl.BlockSpec(memory_space=pltpu.VMEM)],
        out_specs=any_space,
        scratch_shapes=[
            vm((3, CX, 8, CYZ), F32),
            vm((3, CX, 8, CYZ), F32),
            vm((48, 128), F32),
            vm((24 * 216, 128), F32),
            pltpu.SemaphoreType.DMA((2, CX)),
            pltpu.SemaphoreType.DMA((3,)),
        ],
        compiler_params=pltpu.CompilerParams(vmem_limit_bytes=56 << 20),
        name="rotate",
    )(mine, theirs, gram)


def body(orbitals, potential):
    mine, theirs, gram = filter_call(orbitals.reshape(24 * 216, 128), potential.reshape(216, 128))
    return rotate_call(mine, theirs, gram).reshape(orbitals.shape)


def solution(mesh):
    return jax.shard_map(
        body,
        mesh=mesh,
        in_specs=(P("band", "dom", None, None), P("dom", None, None)),
        out_specs=P("band", "dom", None, None),
        check_vma=False,
    )
```

```python
import jax
import jax.numpy as jnp
import numpy as np
from jax import lax
from jax.experimental import pallas as pl
from jax.experimental.pallas import tpu as pltpu
from jax.sharding import PartitionSpec as P

CX = 12
CY = 48
CZ = 48
CYZ = CY * CZ
LANES = 3 * 128 + CYZ + 3 * 128
MESH = pl.DeviceIdType.MESH
BF = jnp.bfloat16
F32 = jnp.float32

stencil_weights = (
    -5369.0 / 1800.0,
    12.0 / 7.0,
    -15.0 / 56.0,
    10.0 / 189.0,
    -1.0 / 112.0,
    2.0 / 1925.0,
    -1.0 / 16632.0,
)
centre_shift = 7.25
half_width = 5.25
near = [-0.5 * w / half_width for w in stencil_weights]
own = (-1.5 * stencil_weights[0] - centre_shift) / half_width


def split_np(a):
    a = a.astype(np.float32)
    high = a.astype(BF)
    return high, (a - high.astype(np.float32)).astype(BF)


def yz_weights():
    out = np.zeros((3, 1280, 256), np.float64)
    for part in range(3):
        for n in range(256):
            cell = 256 * part + n
            row, z = cell // CZ, cell % CZ
            for k in range(1, 7):
                for sign in (-1, 1):
                    out[part, n + 384 + sign * CZ * k, n] += near[k]
                    at = z + sign * k
                    if 0 <= at < CZ:
                        out[part, n + 384 + sign * k, n] += near[k]
                    elif at < 0:
                        out[part, 1024 + row * 6 + at + 6, n] += near[k]
                    else:
                        out[part, 1152 + row * 6 + at - CZ, n] += near[k]
    return split_np(out)


def face_weights():
    out = np.zeros((768, 256), np.float32)
    for row in range(16):
        for i in range(6):
            out[row * CZ + i, row * 6 + i] = 1
            out[row * CZ + CZ - 6 + i, 128 + row * 6 + i] = 1
    return out.astype(BF)


def split(v):
    high = v.astype(BF)
    return high, (v - high.astype(F32)).astype(BF)


def dot(a, b):
    return jnp.dot(a, b, preferred_element_type=F32)


def dot_t(a, b):
    return lax.dot_general(a, b, (((1,), (1,)), ((), ())), preferred_element_type=F32)


def flipped(index, bit):
    return index + bit * (1 - 2 * (index // bit % 2))


def filter_kernel(
    orb, pot_hbm, wh_hbm, wl_hbm, sel_hbm, f_hbm, fo_hbm, gram,
    lin, pot, wh, wl, sel, cen, xrim, zlo, zhi, zlo_out, zhi_out, ylo, yhi, ylo_out, yhi_out, passed, vh, vl, yz, fil, oth, acc, part, got,
    in_sem, out_sem, send_sem, recv_sem, y_send, y_recv, pass_send, band_send, band_recv, sum_send, sum_recv,
):
    band, dom = lax.axis_index("band"), lax.axis_index("dom")
    pairs = [(orb.at[pl.ds(1728 * c, 1728)], lin.at[pl.ds(1728 * c, 1728)]) for c in range(3)]
    pairs = pairs[:1] + [(sel_hbm, sel), (pot_hbm, pot), (wh_hbm, wh), (wl_hbm, wl)] + pairs[1:]
    loads = [pltpu.make_async_copy(a, b, in_sem.at[i]) for i, (a, b) in enumerate(pairs)]
    for load in loads:
        load.start()

    def across(z, core, y, x, other):
        to = dom
        for bit, used in enumerate((core, z % 2, z // 2, y % 2, y // 2, x)):
            if used:
                to = flipped(to, 1 << bit)
        return (1 - band if other else band), to

    stages = [
        [across(k // 2, k % 2, 0, 0, 0) for k in range(1, 8)],
        [across(0, 0, k, 0, 0) for k in range(1, 4)],
        [across(0, 0, 0, k % 2, k // 2) for k in range(1, 4)],
    ]
    partners = [partner for stage in stages for partner in stage]
    barrier = pltpu.get_barrier_semaphore()
    for partner in partners:
        pl.semaphore_signal(barrier, 1, device_id=partner, device_id_type=MESH)

    ends, odds = [], []
    for first in (1, 4, 16):
        odd = (dom // first % 4 + 1) // 2 % 2
        below = odd * flipped(dom, first) + (1 - odd) * flipped(dom, 2 * first)
        above = odd * flipped(dom, 2 * first) + (1 - odd) * flipped(dom, first)
        ends.append(((band, below), (band, above)))
        odds.append(odd)

    def copies(slot, m):
        face = pl.ds(128 * m, 128)
        table = []
        for part in range(2):
            start = 768 * m + 384 * (part * odds[1] + (1 - part) * (1 - odds[1]))
            lanes, centre = pl.ds(start, 384), pl.ds(384 + start, 384)
            table += [
                (cen.at[slot, pl.ds(0, 6), :, centre], xrim.at[slot, 1, :, :, lanes], ends[0][0]),
                (cen.at[slot, pl.ds(6, 6), :, centre], xrim.at[slot, 0, :, :, lanes], ends[0][1]),
            ]
        table += [
            (zlo_out.at[slot, :, :, face], zhi.at[slot, :, :, face], ends[2][0]),
            (zhi_out.at[slot, :, :, face], zlo.at[slot, :, :, face], ends[2][1]),
        ]
        return [
            pltpu.make_async_remote_copy(
                a, b, send_sem.at[slot, m, i], recv_sem.at[slot, m, i], device_id=to, device_id_type=MESH
            )
            for i, (a, b, to) in enumerate(table)
        ]

    def y_moves(slot, face, half, sources, sems, to):
        rim = cen.at[slot, pl.ds(6 * half, 6), :, pl.ds((384 + CYZ, 128)[face], 256)]
        return [
            pltpu.make_async_remote_copy(
                a, b, sems[i], y_recv.at[slot, face, half, i], device_id=to, device_id_type=MESH
            )
            for i, (a, b) in enumerate(zip(sources, (rim, (yhi, ylo)[face].at[slot, half])))
        ]

    def y_copies(slot, face, half):
        sources = (
            cen.at[slot, pl.ds(6 * half, 6), :, pl.ds((384, 128 + CYZ)[face], 256)],
            (ylo_out, yhi_out)[face].at[slot, half],
        )
        sems = [y_send.at[slot, face, half, i] for i in range(2)]
        return y_moves(slot, face, half, sources, sems, ends[1][face])

    def forward_copies(slot, face):
        sources = (xrim.at[slot, odds[0], :, :, pl.ds((0, CYZ - 256)[face], 256)], passed.at[slot])
        sems = [pass_send.at[slot, i] for i in range(2)]
        return y_moves(slot, face, 1 - odds[0], sources, sems, (band, flipped(flipped(dom, 2), 4)))

    def band_copy(chunk, m, half):
        part_of = (chunk, pl.ds(6 * half, 6), slice(None), pl.ds(768 * m, 768))
        return pltpu.make_async_remote_copy(
            fil.at[part_of], oth.at[part_of], band_send.at[chunk, m, half], band_recv.at[chunk, m, half],
            device_id=(1 - band, dom), device_id_type=MESH,
        )

    lane = lax.broadcasted_iota(jnp.int32, (8, 128), 1)

    def group(i):
        return 2 - i + odds[1] * (2 * i - 2)

    def packed(tiles, shift):
        v = [pltpu.roll(tile, (32 * (q % 4) + shift) % 128, 1) for q, tile in enumerate(tiles)]
        first = jnp.where(lane < 64, jnp.where(lane < 32, v[0], v[1]), jnp.where(lane < 96, v[2], v[3]))
        return first, jnp.where(lane < 32, v[4], v[5])

    def for_outer(face, act):
        @pl.when(odds[1] == face)
        def _():
            act()

    def send_y(slot, face):
        start, shift = ((640, 0), (CYZ, 32))[face]
        for half in range(2):
            tiles = [cen[slot, 6 * half + q, :, pl.ds(start, 128)] for q in range(6)]
            out = (ylo_out, yhi_out)[face]
            out[slot, half, 0], out[slot, half, 1] = packed(tiles, shift)

        def start_outer():
            for copy in y_copies(slot, face, odds[0]):
                copy.start()

        for copy in y_copies(slot, face, 1 - odds[0]):
            copy.start()
        for_outer(face, start_outer)

    def forward(slot):
        for face in range(2):

            @pl.when(odds[1] == 1 - face)
            def _():
                start, shift = ((256, 0), (CYZ - 384, 32))[face]
                tiles = [xrim[slot, odds[0], q, :, pl.ds(start, 128)] for q in range(6)]
                passed[slot, 0], passed[slot, 1] = packed(tiles, shift)
                for copy in forward_copies(slot, face):
                    copy.start()

    def prepare(slot, m):
        lanes = pl.ds(pl.multiple_of(384 + 768 * m, 128), 768)
        face = pl.ds(pl.multiple_of(128 * m, 128), 128)
        high, low = split(cen[slot, :, :, lanes].reshape(96, 768))
        vh[slot, :, lanes] = high
        vl[slot, :, lanes] = low
        faces = dot(high, sel[...]) + dot(low, sel[...])
        for out, at in ((zlo_out, 0), (zhi_out, 128)):
            f = faces[:, at : at + 128].reshape(CX, 8, 128)
            for x in range(9):
                last = pltpu.roll(f[x // 3 * 4 + 3], 96 - 32 * (x % 3), 1)
                out[slot, x, :, face] = jnp.where(lane < 96, f[x // 3 * 4 + x % 3], last)

    def send(slot, m, first, count):
        for copy in copies(slot, m)[first : first + count]:
            copy.start()

    def split_rim(slot, face, rim, start, at, shift):
        for half in range(2):
            for copy in y_copies(slot, face, half):
                copy.wait_recv()
        for x in range(CX):
            tile = rim[slot, x // 6, x % 6 // 4]
            cen[slot, x, :, pl.ds(at, 128)] = pltpu.roll(tile, (shift - 32 * (x % 6 % 4)) % 128, 1)
        high, low = split(cen[slot, :, :, pl.ds(start, 384)].reshape(96, 384))
        vh[slot, :, pl.ds(start, 384)] = high
        vl[slot, :, pl.ds(start, 384)] = low

    def receive_y(slot, m):
        @pl.when(m == 0)
        def _():
            split_rim(slot, 1, ylo, 0, 0, 96)

        @pl.when(m == 2)
        def _():
            split_rim(slot, 0, yhi, 384 + CYZ, 640 + CYZ, 0)

    def receive(slot, m, first, count):
        for copy in copies(slot, m)[first : first + count]:
            copy.wait_recv()

    def arrive(slot, m, i, meanwhile):
        @pl.when(i == 0)
        def _():
            receive(slot, m, 0, 2)
            forward(slot)

        receive_y(slot, m)
        yz_product(slot, m)
        meanwhile()

        @pl.when(i > 0)
        def _():
            receive(slot, m, 0, 2)

        receive(slot, m, 2, 4)

    def z_rim(rim, slot, face):
        out = []
        for g in range(3):
            v = [rim[slot, 3 * g + q, :, face] for q in range(3)]
            r = [pltpu.roll(v[q], 32 + 32 * q, 1) for q in range(3)]
            out += v + [jnp.where(lane < 32, r[0], jnp.where(lane < 64, r[1], r[2]))]
        return jnp.concatenate(out, 0)

    def yz_product(slot, m):
        for j in range(3):
            window = pl.ds(pl.multiple_of(256 * j + 768 * m, 256), 1024)
            high, low = vh[slot, :, window], vl[slot, :, window]
            wide = dot(high, wh[j, 0:1024]) + dot(low, wh[j, 0:1024]) + dot(high, wl[j, 0:1024])
            yz[:, pl.ds(256 * j, 256)] = wide

    def rim_product(slot, m):
        face = pl.ds(pl.multiple_of(128 * m, 128), 128)
        high, low = split(jnp.concatenate([z_rim(zlo, slot, face), z_rim(zhi, slot, face)], 1))
        for j in range(3):
            rims = slice(1024, 1280)
            yz[:, pl.ds(256 * j, 256)] += dot(high, wh[j, rims]) + dot(low, wh[j, rims]) + dot(high, wl[j, rims])

    def stencil(slot, m, write):
        @pl.loop(0, 6)
        def _(t):
            at = pl.multiple_of(768 * m + 128 * t, 128)
            here, mid = pl.ds(at, 128), pl.ds(pl.multiple_of(at + 384, 128), 128)
            v = [xrim[slot, 0, i, :, here] for i in range(6)]
            v += [cen[slot, i, :, mid] for i in range(CX)]
            v += [xrim[slot, 1, i, :, here] for i in range(6)]
            for x in range(CX):
                diagonal = pot[pl.ds(18 * x + 6 * m + t, 1), :] * (1.0 / half_width) + own
                total = diagonal * v[x + 6] + yz[pl.ds(8 * x, 8), pl.ds(pl.multiple_of(128 * t, 128), 128)]
                for k in range(1, 7):
                    total = total + near[k] * (v[x + 6 - k] + v[x + 6 + k])
                write(x, here, mid, total)

    def relayout(chunk, m):
        for x in range(CX):
            for t in range(6):
                row = 8 * 216 * chunk + 18 * x + 6 * m + t
                lanes = pl.ds(pl.multiple_of(384 + 768 * m + 128 * t, 128), 128)
                cen[chunk, x, :, lanes] = lin[pl.ds(row, 8, stride=216), :]

    def rows(ref, m, first, layers):
        lanes = pl.ds(pl.multiple_of(768 * m, 128), 768)
        pieces = [split(ref[:, first + x, :, lanes].reshape(24, 768)) for x in range(layers)]
        return jnp.concatenate([jnp.concatenate([p[i] for p in pieces], 1) for i in range(2)], 0)

    def folded(a, b):
        products = dot_t(a, b)
        return products[:24, :24] + products[24:, :24] + products[:24, 24:]

    def own_products(m):
        a = rows(fil, m, 0, CX)
        acc[:, 0:24] += folded(a, a)

    def enter(chunk):
        @pl.loop(0, 3)
        def _(i):
            relayout(chunk, group(i))

        if chunk > 0:

            @pl.loop(0, 3)
            def _(i):
                prepare(chunk, group(i))
                send(chunk, group(i), 4, 2)

    def fil_out(chunk):
        return pltpu.make_async_copy(fil.at[chunk], f_hbm.at[chunk], out_sem.at[chunk])

    def oth_out(chunk):
        return pltpu.make_async_copy(oth.at[chunk], fo_hbm.at[chunk], out_sem.at[3 + chunk])

    def last_out(half):
        layers = pl.ds(6 * half, 6)
        return pltpu.make_async_copy(oth.at[2, layers], fo_hbm.at[2, layers], out_sem.at[5 + half])

    acc[...] = jnp.zeros_like(acc)
    loads[0].wait()
    loads[1].wait()
    enter(0)
    pl.semaphore_wait(barrier, len(partners))
    send(0, group(0), 0, 4)
    send_y(0, 0)
    send_y(0, 1)

    @pl.loop(0, 3)
    def _(i):
        @pl.when(i > 0)
        def _():
            send(0, group(i), 0, 4)

        prepare(0, group(i))
        send(0, group(i), 4, 2)

    for load in loads[2:]:
        load.wait()
    enter(1)

    @pl.loop(0, 3)
    def _(chunk):
        @pl.loop(0, 3)
        def _(i):
            m, slot = group(i), chunk

            def meanwhile():
                @pl.when((band == 0) & (chunk > 0))
                def _():
                    band_copy(chunk - 1, m, 0).start()

            arrive(slot, m, i, meanwhile)
            rim_product(slot, m)

            def write(x, here, mid, total):
                cen[chunk + 3, x, :, mid] = total

            stencil(slot, m, write)

            send(slot + 3, m, 0, 4)

            @pl.when(m == 0)
            def _():
                send_y(slot + 3, 0)

            @pl.when(m == 2)
            def _():
                send_y(slot + 3, 1)

            prepare(slot + 3, m)
            send(slot + 3, m, 4, 2)

        @pl.when(chunk == 0)
        def _():
            enter(2)

        @pl.when(chunk < 2)
        def _():
            send_y(chunk + 1, 0)
            send_y(chunk + 1, 1)

        @pl.loop(0, 3)
        def _(i):
            m, slot = group(i), chunk + 3
            arrive(slot, m, i, lambda: None)

            @pl.when(chunk < 2)
            def _():
                send(chunk + 1, m, 0, 4)

            rim_product(slot, m)

            def write(x, here, mid, total):
                fil[chunk, x, :, here] = 2.0 * total - cen[chunk, x, :, mid]

            stencil(slot, m, write)
            band_copy(chunk, m, 1 - band).start()

            @pl.when(chunk == 2)
            def _():
                own_products(m)

        fil_out(chunk).start()

    def cross_products(m):
        for chunk in range(3):
            band_copy(chunk, m, band).wait_recv()
        mine, theirs = rows(fil, m, 6 * band, 6), rows(oth, m, 6 * band, 6)
        first, second = jnp.where(band == 0, mine, theirs), jnp.where(band == 0, theirs, mine)
        acc[:, 64:88] += folded(second, first)

    @pl.loop(0, 3)
    def _(i):
        @pl.when(i == 2)
        def _():
            for m in range(3):
                band_copy(2, m, 1 - band).wait_send()

            @pl.when(band == 0)
            def _():
                for m in range(3):
                    band_copy(2, m, 0).start()

        cross_products(group(i))

    v = acc[...]
    alone = jnp.where(lax.broadcasted_iota(jnp.int32, (24, 128), 1) < 24, v, 0.0)
    cross = v - alone
    tail = pltpu.roll(alone[16:], 72, 1)
    part[0] = (
        jnp.where(band == 0, alone[:16], pltpu.roll(alone[:16], 24, 1))
        + pltpu.roll(cross[:16], 112, 1)
        + jnp.concatenate([jnp.where(band == 0, tail, 0.0) + pltpu.roll(cross[16:], 32, 1), jnp.where(band == 0, 0.0, tail)], 0)
    )

    def settle_early():
        @pl.when(band == 1)
        def _():
            last_out(1).start()

            @pl.loop(0, 2)
            def _(chunk):
                for m in range(3):
                    band_copy(chunk, m, 0).wait_recv()
                oth_out(chunk).start()

        @pl.loop(0, 6)
        def _(slot):
            for m in range(3):
                for copy in copies(slot, m):
                    copy.wait_send()
            for face in range(2):

                def wait_outer():
                    for copy in y_copies(slot, face, odds[0]):
                        copy.wait_send()

                for copy in y_copies(slot, face, 1 - odds[0]):
                    copy.wait_send()
                for_outer(face, wait_outer)
            for copy in forward_copies(slot, 0):
                copy.wait_send()

    def settle_late():
        @pl.loop(0, 2)
        def _(chunk):
            for m in range(3):
                band_copy(chunk, m, 1 - band).wait_send()

            @pl.when(band == 0)
            def _():
                for m in range(3):
                    band_copy(chunk, m, 0).wait_send()

            @pl.when(band == 1)
            def _():
                oth_out(chunk).wait()

        for chunk in range(3):
            fil_out(chunk).wait()

        @pl.when(band == 0)
        def _():
            for m in range(3):
                band_copy(2, m, 0).wait_send()

        @pl.when(band == 1)
        def _():
            for m in range(3):
                band_copy(2, m, 0).wait_recv()
            last_out(0).start()
            last_out(1).wait()

    index = 0
    for number, stage in enumerate(stages):
        moves = []
        for partner in stage:
            moves.append(
                pltpu.make_async_remote_copy(
                    part.at[number], got.at[index], sum_send.at[index], sum_recv.at[index],
                    device_id=partner, device_id_type=MESH,
                )
            )
            index += 1
        for move in moves:
            move.start()
        (settle_early, lambda: None, settle_late)[number]()
        for move in moves:
            move.wait_recv()
        terms = [part[number]] + [got[index - len(stage) + k] for k in range(len(stage))]
        while len(terms) > 1:
            terms = [a + b for a, b in zip(terms[::2], terms[1::2])]
        if number < 2:
            part[number + 1] = terms[0]
        else:
            gram[...] = terms[0]
        for move in moves:
            move.wait_send()

    @pl.when(band == 1)
    def _():
        last_out(0).wait()


def filter_call(lines, pot):
    wh, wl = yz_weights()
    sel = face_weights()
    any_space = pl.BlockSpec(memory_space=pl.ANY)
    chunk = (3, CX, 8, CYZ)
    vm = pltpu.VMEM
    return pl.pallas_call(
        filter_kernel,
        out_shape=(
            jax.ShapeDtypeStruct(chunk, F32),
            jax.ShapeDtypeStruct(chunk, F32),
            jax.ShapeDtypeStruct((16, 128), F32),
        ),
        in_specs=[any_space] * 5,
        out_specs=(any_space, any_space, pl.BlockSpec(memory_space=pltpu.VMEM)),
        scratch_shapes=[
            vm((24 * 216, 128), F32),
            vm((216, 128), F32),
            vm(wh.shape, BF),
            vm(wl.shape, BF),
            vm(sel.shape, BF),
            vm((6, CX, 8, LANES), F32),
            vm((6, 2, 6, 8, CYZ), F32),
            vm((6, 9, 8, 384), F32),
            vm((6, 9, 8, 384), F32),
            vm((6, 9, 8, 384), F32),
            vm((6, 9, 8, 384), F32),
            vm((6, 2, 2, 8, 128), F32),
            vm((6, 2, 2, 8, 128), F32),
            vm((6, 2, 2, 8, 128), F32),
            vm((6, 2, 2, 8, 128), F32),
            vm((6, 2, 8, 128), F32),
            vm((6, 96, LANES), BF),
            vm((6, 96, LANES), BF),
            vm((96, 768), F32),
            vm(chunk, F32),
            vm(chunk, F32),
            vm((24, 128), F32),
            vm((3, 16, 128), F32),
            vm((13, 16, 128), F32),
            pltpu.SemaphoreType.DMA((7,)),
            pltpu.SemaphoreType.DMA((7,)),
            pltpu.SemaphoreType.DMA((6, 3, 6)),
            pltpu.SemaphoreType.DMA((6, 3, 6)),
            pltpu.SemaphoreType.DMA((6, 2, 2, 2)),
            pltpu.SemaphoreType.DMA((6, 2, 2, 2)),
            pltpu.SemaphoreType.DMA((6, 2)),
            pltpu.SemaphoreType.DMA((3, 3, 2)),
            pltpu.SemaphoreType.DMA((3, 3, 2)),
            pltpu.SemaphoreType.DMA((13,)),
            pltpu.SemaphoreType.DMA((13,)),
        ],
        compiler_params=pltpu.CompilerParams(collective_id=0, has_side_effects=True, vmem_limit_bytes=56 << 20),
        name="filter",
    )(lines, pot, jnp.asarray(wh), jnp.asarray(wl), jnp.asarray(sel))


def rotate_kernel(low, high, gram, out, mine, theirs, inverse, lines, sems, out_sems):
    band = lax.axis_index("band")

    def loads(x):
        own_load = pltpu.make_async_copy(low.at[:, x], mine.at[:, x], sems.at[0, x])
        return own_load, pltpu.make_async_copy(high.at[:, x], theirs.at[:, x], sems.at[1, x])

    for x in range(CX):
        loads(x)[0].start()

        @pl.when(band == 1)
        def _():
            loads(x)[1].start()

    g = gram[...] * (1.0 / (64 * CX * CYZ))
    blank = jnp.zeros((24, 16), F32)
    row, col = (lax.broadcasted_iota(jnp.int32, (48, 64), d) for d in range(2))
    unit = (row == col).astype(F32)
    first = jnp.concatenate([g[:, 0:24], g[0:8, 72:96]], 0)
    second = jnp.concatenate([g[:, 24:48], g[8:16, 72:96]], 0)
    cross = jnp.concatenate([g[:, 48:72], g[0:8, 96:120]], 0)
    turned = lax.dot_general(unit[:24, :24], cross, (((1,), (1,)), ((), ())), precision=lax.Precision.HIGHEST)
    left = jnp.concatenate(
        [jnp.concatenate([first, turned, blank], 1), jnp.concatenate([cross, second, blank], 1)], 0
    )
    table = jnp.concatenate([left, unit], 1)
    rows = lax.broadcasted_iota(jnp.int32, (48, 128), 0)
    for k in range(0, 48, 2):
        one = jnp.broadcast_to(table[:, k : k + 1], (48, 128))
        two = jnp.broadcast_to(table[:, k + 1 : k + 2], (48, 128))
        a, b, c = one[k : k + 1], one[k + 1 : k + 2], two[k + 1 : k + 2]
        upper, lower = table[k : k + 1], table[k + 1 : k + 2]
        inverse[k : k + 1, :] = upper * lax.rsqrt(a)
        ratio = b / a
        inverse[k + 1 : k + 2, :] = (lower - ratio * upper) * lax.rsqrt(c - ratio * b)
        if k < 46:
            scale = 1.0 / (a * c - b * b)
            below = rows > k + 1
            table = (
                table
                - jnp.where(below, one, 0.0) * ((c * upper - b * lower) * scale)
                - jnp.where(below, two, 0.0) * ((a * lower - b * upper) * scale)
            )

    def sent(quarter):
        at = pl.ds(72 * quarter, 72)
        return pltpu.make_async_copy(lines.reshape(24, 216, 128).at[:, at], out.at[:, at], out_sems.at[quarter])

    def rotate(matrix, sources):
        mh, ml = split(matrix)
        left = jnp.concatenate([jnp.concatenate([mh, mh], 1), jnp.concatenate([ml, jnp.zeros_like(ml)], 1)], 0)
        for x in range(CX):
            for load in loads(x)[: len(sources)]:
                load.wait()
            v = [source[:, x].reshape(24, CYZ) for source in sources]
            vh, vl = split(jnp.concatenate(v, 0) if len(v) > 1 else v[0])
            made = dot(left, jnp.concatenate([vh, vl], 0))
            made = made[:24] + made[24:]
            for t in range(18):
                lines[pl.ds(18 * x + t, 24, stride=216), :] = made[:, 128 * t : 128 * t + 128]
            if x % 4 == 3:
                sent(x // 4).start()

    @pl.when(band == 0)
    def _():
        rotate(inverse[0:24, 64:88], [mine])

    @pl.when(band == 1)
    def _():
        rotate(jnp.concatenate([inverse[24:48, 88:112], inverse[24:48, 64:88]], 1), [mine, theirs])

    for quarter in range(3):
        sent(quarter).wait()


def rotate_call(mine, theirs, gram):
    any_space = pl.BlockSpec(memory_space=pl.ANY)
    vm = pltpu.VMEM
    return pl.pallas_call(
        rotate_kernel,
        out_shape=jax.ShapeDtypeStruct((24, 216, 128), F32),
        in_specs=[any_space, any_space, pl.BlockSpec(memory_space=pltpu.VMEM)],
        out_specs=any_space,
        scratch_shapes=[
            vm((3, CX, 8, CYZ), F32),
            vm((3, CX, 8, CYZ), F32),
            vm((48, 128), F32),
            vm((24 * 216, 128), F32),
            pltpu.SemaphoreType.DMA((2, CX)),
            pltpu.SemaphoreType.DMA((3,)),
        ],
        compiler_params=pltpu.CompilerParams(vmem_limit_bytes=56 << 20),
        name="rotate",
    )(mine, theirs, gram)


def body(orbitals, potential):
    mine, theirs, gram = filter_call(orbitals.reshape(24 * 216, 128), potential.reshape(216, 128))
    return rotate_call(mine, theirs, gram).reshape(orbitals.shape)


def solution(mesh):
    return jax.shard_map(
        body,
        mesh=mesh,
        in_specs=(P("band", "dom", None, None), P("dom", None, None)),
        out_specs=P("band", "dom", None, None),
        check_vma=False,
    )
```

```python
import jax
import jax.numpy as jnp
import numpy as np
from jax import lax
from jax.experimental import pallas as pl
from jax.experimental.pallas import tpu as pltpu
from jax.sharding import PartitionSpec as P

CX = 12
CY = 48
CZ = 48
CYZ = CY * CZ
LANES = 3 * 128 + CYZ + 3 * 128
MESH = pl.DeviceIdType.MESH
BF = jnp.bfloat16
F32 = jnp.float32

stencil_weights = (
    -5369.0 / 1800.0,
    12.0 / 7.0,
    -15.0 / 56.0,
    10.0 / 189.0,
    -1.0 / 112.0,
    2.0 / 1925.0,
    -1.0 / 16632.0,
)
centre_shift = 7.25
half_width = 5.25
near = [-0.5 * w / half_width for w in stencil_weights]
own = (-1.5 * stencil_weights[0] - centre_shift) / half_width


def split_np(a):
    a = a.astype(np.float32)
    high = a.astype(BF)
    return high, (a - high.astype(np.float32)).astype(BF)


def yz_weights():
    out = np.zeros((3, 1280, 256), np.float64)
    for part in range(3):
        for n in range(256):
            cell = 256 * part + n
            row, z = cell // CZ, cell % CZ
            for k in range(1, 7):
                for sign in (-1, 1):
                    out[part, n + 384 + sign * CZ * k, n] += near[k]
                    at = z + sign * k
                    if 0 <= at < CZ:
                        out[part, n + 384 + sign * k, n] += near[k]
                    elif at < 0:
                        out[part, 1024 + row * 6 + at + 6, n] += near[k]
                    else:
                        out[part, 1152 + row * 6 + at - CZ, n] += near[k]
    return split_np(out)


def face_weights():
    out = np.zeros((768, 256), np.float32)
    for row in range(16):
        for i in range(6):
            out[row * CZ + i, row * 6 + i] = 1
            out[row * CZ + CZ - 6 + i, 128 + row * 6 + i] = 1
    return out.astype(BF)


def split(v):
    high = v.astype(BF)
    return high, (v - high.astype(F32)).astype(BF)


def dot(a, b):
    return jnp.dot(a, b, preferred_element_type=F32)


def dot_t(a, b):
    return lax.dot_general(a, b, (((1,), (1,)), ((), ())), preferred_element_type=F32)


def flipped(index, bit):
    return index + bit * (1 - 2 * (index // bit % 2))


def filter_kernel(
    orb, pot_hbm, wh_hbm, wl_hbm, sel_hbm, f_hbm, fo_hbm, gram,
    lin, pot, wh, wl, sel, cen, xrim, zlo, zhi, zlo_out, zhi_out, ylo, yhi, ylo_out, yhi_out, passed, vh, vl, yz, fil, oth, acc, part, got,
    in_sem, out_sem, send_sem, recv_sem, y_send, y_recv, pass_send, band_send, band_recv, sum_send, sum_recv,
):
    band, dom = lax.axis_index("band"), lax.axis_index("dom")
    pairs = [(orb.at[pl.ds(1728 * c, 1728)], lin.at[pl.ds(1728 * c, 1728)]) for c in range(3)]
    pairs = pairs[:1] + [(sel_hbm, sel), (pot_hbm, pot), (wh_hbm, wh), (wl_hbm, wl)] + pairs[1:]
    loads = [pltpu.make_async_copy(a, b, in_sem.at[i]) for i, (a, b) in enumerate(pairs)]
    for load in loads:
        load.start()

    def across(z, core, y, x, other):
        to = dom
        for bit, used in enumerate((core, z % 2, z // 2, y % 2, y // 2, x)):
            if used:
                to = flipped(to, 1 << bit)
        return (1 - band if other else band), to

    stages = [
        [across(k // 2, k % 2, 0, 0, 0) for k in range(1, 8)],
        [across(0, 0, k, 0, 0) for k in range(1, 4)],
        [across(0, 0, 0, k % 2, k // 2) for k in range(1, 4)],
    ]
    partners = [partner for stage in stages for partner in stage]
    barrier = pltpu.get_barrier_semaphore()
    for partner in partners:
        pl.semaphore_signal(barrier, 1, device_id=partner, device_id_type=MESH)

    ends, odds = [], []
    for first in (1, 4, 16):
        odd = (dom // first % 4 + 1) // 2 % 2
        below = odd * flipped(dom, first) + (1 - odd) * flipped(dom, 2 * first)
        above = odd * flipped(dom, 2 * first) + (1 - odd) * flipped(dom, first)
        ends.append(((band, below), (band, above)))
        odds.append(odd)

    def copies(slot, m):
        face = pl.ds(128 * m, 128)
        table = []
        for part in range(2):
            start = 768 * m + 384 * (part * odds[1] + (1 - part) * (1 - odds[1]))
            lanes, centre = pl.ds(start, 384), pl.ds(384 + start, 384)
            table += [
                (cen.at[slot, pl.ds(0, 6), :, centre], xrim.at[slot, 1, :, :, lanes], ends[0][0]),
                (cen.at[slot, pl.ds(6, 6), :, centre], xrim.at[slot, 0, :, :, lanes], ends[0][1]),
            ]
        table += [
            (zlo_out.at[slot, :, :, face], zhi.at[slot, :, :, face], ends[2][0]),
            (zhi_out.at[slot, :, :, face], zlo.at[slot, :, :, face], ends[2][1]),
        ]
        return [
            pltpu.make_async_remote_copy(
                a, b, send_sem.at[slot, m, i], recv_sem.at[slot, m, i], device_id=to, device_id_type=MESH
            )
            for i, (a, b, to) in enumerate(table)
        ]

    def y_moves(slot, face, half, sources, sems, to):
        rim = cen.at[slot, pl.ds(6 * half, 6), :, pl.ds((384 + CYZ, 128)[face], 256)]
        return [
            pltpu.make_async_remote_copy(
                a, b, sems[i], y_recv.at[slot, face, half, i], device_id=to, device_id_type=MESH
            )
            for i, (a, b) in enumerate(zip(sources, (rim, (yhi, ylo)[face].at[slot, half])))
        ]

    def y_copies(slot, face, half):
        sources = (
            cen.at[slot, pl.ds(6 * half, 6), :, pl.ds((384, 128 + CYZ)[face], 256)],
            (ylo_out, yhi_out)[face].at[slot, half],
        )
        sems = [y_send.at[slot, face, half, i] for i in range(2)]
        return y_moves(slot, face, half, sources, sems, ends[1][face])

    def forward_copies(slot, face):
        sources = (xrim.at[slot, odds[0], :, :, pl.ds((0, CYZ - 256)[face], 256)], passed.at[slot])
        sems = [pass_send.at[slot, i] for i in range(2)]
        return y_moves(slot, face, 1 - odds[0], sources, sems, (band, flipped(flipped(dom, 2), 4)))

    def band_copy(chunk, m, half):
        part_of = (chunk, pl.ds(6 * half, 6), slice(None), pl.ds(768 * m, 768))
        return pltpu.make_async_remote_copy(
            fil.at[part_of], oth.at[part_of], band_send.at[chunk, m, half], band_recv.at[chunk, m, half],
            device_id=(1 - band, dom), device_id_type=MESH,
        )

    lane = lax.broadcasted_iota(jnp.int32, (8, 128), 1)

    def group(i):
        return 2 - i + odds[1] * (2 * i - 2)

    def packed(tiles, shift):
        v = [pltpu.roll(tile, (32 * (q % 4) + shift) % 128, 1) for q, tile in enumerate(tiles)]
        first = jnp.where(lane < 64, jnp.where(lane < 32, v[0], v[1]), jnp.where(lane < 96, v[2], v[3]))
        return first, jnp.where(lane < 32, v[4], v[5])

    def for_outer(face, act):
        @pl.when(odds[1] == face)
        def _():
            act()

    def send_y(slot, face):
        start, shift = ((640, 0), (CYZ, 32))[face]
        for half in range(2):
            tiles = [cen[slot, 6 * half + q, :, pl.ds(start, 128)] for q in range(6)]
            out = (ylo_out, yhi_out)[face]
            out[slot, half, 0], out[slot, half, 1] = packed(tiles, shift)

        def start_outer():
            for copy in y_copies(slot, face, odds[0]):
                copy.start()

        for copy in y_copies(slot, face, 1 - odds[0]):
            copy.start()
        for_outer(face, start_outer)

    def forward(slot):
        for face in range(2):

            @pl.when(odds[1] == 1 - face)
            def _():
                start, shift = ((256, 0), (CYZ - 384, 32))[face]
                tiles = [xrim[slot, odds[0], q, :, pl.ds(start, 128)] for q in range(6)]
                passed[slot, 0], passed[slot, 1] = packed(tiles, shift)
                for copy in forward_copies(slot, face):
                    copy.start()

    def prepare(slot, m):
        lanes = pl.ds(pl.multiple_of(384 + 768 * m, 128), 768)
        face = pl.ds(pl.multiple_of(128 * m, 128), 128)
        high, low = split(cen[slot, :, :, lanes].reshape(96, 768))
        vh[slot, :, lanes] = high
        vl[slot, :, lanes] = low
        faces = dot(high, sel[...]) + dot(low, sel[...])
        for out, at in ((zlo_out, 0), (zhi_out, 128)):
            f = faces[:, at : at + 128].reshape(CX, 8, 128)
            for x in range(9):
                last = pltpu.roll(f[x // 3 * 4 + 3], 96 - 32 * (x % 3), 1)
                out[slot, x, :, face] = jnp.where(lane < 96, f[x // 3 * 4 + x % 3], last)

    def send(slot, m, first, count):
        for copy in copies(slot, m)[first : first + count]:
            copy.start()

    def split_rim(slot, face, rim, start, at, shift):
        for half in range(2):
            for copy in y_copies(slot, face, half):
                copy.wait_recv()
        for x in range(CX):
            tile = rim[slot, x // 6, x % 6 // 4]
            cen[slot, x, :, pl.ds(at, 128)] = pltpu.roll(tile, (shift - 32 * (x % 6 % 4)) % 128, 1)
        high, low = split(cen[slot, :, :, pl.ds(start, 384)].reshape(96, 384))
        vh[slot, :, pl.ds(start, 384)] = high
        vl[slot, :, pl.ds(start, 384)] = low

    def receive_y(slot, m):
        @pl.when(m == 0)
        def _():
            split_rim(slot, 1, ylo, 0, 0, 96)

        @pl.when(m == 2)
        def _():
            split_rim(slot, 0, yhi, 384 + CYZ, 640 + CYZ, 0)

    def receive(slot, m, first, count):
        for copy in copies(slot, m)[first : first + count]:
            copy.wait_recv()

    def arrive(slot, m, i, meanwhile):
        @pl.when(i == 0)
        def _():
            receive(slot, m, 0, 2)
            forward(slot)

        receive_y(slot, m)
        yz_product(slot, m)
        meanwhile()

        @pl.when(i > 0)
        def _():
            receive(slot, m, 0, 2)

        receive(slot, m, 2, 4)

    def z_rim(rim, slot, face):
        out = []
        for g in range(3):
            v = [rim[slot, 3 * g + q, :, face] for q in range(3)]
            r = [pltpu.roll(v[q], 32 + 32 * q, 1) for q in range(3)]
            out += v + [jnp.where(lane < 32, r[0], jnp.where(lane < 64, r[1], r[2]))]
        return jnp.concatenate(out, 0)

    def yz_product(slot, m):
        for j in range(3):
            window = pl.ds(pl.multiple_of(256 * j + 768 * m, 256), 1024)
            high, low = vh[slot, :, window], vl[slot, :, window]
            wide = dot(high, wh[j, 0:1024]) + dot(low, wh[j, 0:1024]) + dot(high, wl[j, 0:1024])
            yz[:, pl.ds(256 * j, 256)] = wide

    def rim_product(slot, m):
        face = pl.ds(pl.multiple_of(128 * m, 128), 128)
        high, low = split(jnp.concatenate([z_rim(zlo, slot, face), z_rim(zhi, slot, face)], 1))
        for j in range(3):
            rims = slice(1024, 1280)
            yz[:, pl.ds(256 * j, 256)] += dot(high, wh[j, rims]) + dot(low, wh[j, rims]) + dot(high, wl[j, rims])

    def stencil(slot, m, write):
        @pl.loop(0, 6)
        def _(t):
            at = pl.multiple_of(768 * m + 128 * t, 128)
            here, mid = pl.ds(at, 128), pl.ds(pl.multiple_of(at + 384, 128), 128)
            v = [xrim[slot, 0, i, :, here] for i in range(6)]
            v += [cen[slot, i, :, mid] for i in range(CX)]
            v += [xrim[slot, 1, i, :, here] for i in range(6)]
            for x in range(CX):
                diagonal = pot[pl.ds(18 * x + 6 * m + t, 1), :] * (1.0 / half_width) + own
                total = diagonal * v[x + 6] + yz[pl.ds(8 * x, 8), pl.ds(pl.multiple_of(128 * t, 128), 128)]
                for k in range(1, 7):
                    total = total + near[k] * (v[x + 6 - k] + v[x + 6 + k])
                write(x, here, mid, total)

    def relayout(chunk, m):
        for x in range(CX):
            for t in range(6):
                row = 8 * 216 * chunk + 18 * x + 6 * m + t
                lanes = pl.ds(pl.multiple_of(384 + 768 * m + 128 * t, 128), 128)
                cen[chunk, x, :, lanes] = lin[pl.ds(row, 8, stride=216), :]

    def rows(ref, m, first, layers):
        lanes = pl.ds(pl.multiple_of(768 * m, 128), 768)
        pieces = [split(ref[:, first + x, :, lanes].reshape(24, 768)) for x in range(layers)]
        return jnp.concatenate([jnp.concatenate([p[i] for p in pieces], 1) for i in range(2)], 0)

    def folded(a, b):
        products = dot_t(a, b)
        return products[:24, :24] + products[24:, :24] + products[:24, 24:]

    def own_products(m):
        a = rows(fil, m, 0, CX)
        acc[:, 0:24] += folded(a, a)

    def enter(chunk):
        @pl.loop(0, 3)
        def _(i):
            relayout(chunk, group(i))

        if chunk > 0:

            @pl.loop(0, 3)
            def _(i):
                prepare(chunk, group(i))
                send(chunk, group(i), 4, 2)

    def fil_out(chunk):
        return pltpu.make_async_copy(fil.at[chunk], f_hbm.at[chunk], out_sem.at[chunk])

    def oth_out(chunk):
        return pltpu.make_async_copy(oth.at[chunk], fo_hbm.at[chunk], out_sem.at[3 + chunk])

    def last_out(half):
        layers = pl.ds(6 * half, 6)
        return pltpu.make_async_copy(oth.at[2, layers], fo_hbm.at[2, layers], out_sem.at[5 + half])

    acc[...] = jnp.zeros_like(acc)
    loads[0].wait()
    loads[1].wait()
    enter(0)
    pl.semaphore_wait(barrier, len(partners))
    send(0, group(0), 0, 4)
    send_y(0, 0)
    send_y(0, 1)

    @pl.loop(0, 3)
    def _(i):
        @pl.when(i > 0)
        def _():
            send(0, group(i), 0, 4)

        prepare(0, group(i))
        send(0, group(i), 4, 2)

    for load in loads[2:]:
        load.wait()
    enter(1)

    @pl.loop(0, 3)
    def _(chunk):
        @pl.loop(0, 3)
        def _(i):
            m, slot = group(i), chunk

            def meanwhile():
                @pl.when((band == 0) & (chunk > 0))
                def _():
                    band_copy(chunk - 1, m, 0).start()

            arrive(slot, m, i, meanwhile)
            rim_product(slot, m)

            def write(x, here, mid, total):
                cen[chunk + 3, x, :, mid] = total

            stencil(slot, m, write)

            send(slot + 3, m, 0, 4)

            @pl.when(m == 0)
            def _():
                send_y(slot + 3, 0)

            @pl.when(m == 2)
            def _():
                send_y(slot + 3, 1)

            prepare(slot + 3, m)
            send(slot + 3, m, 4, 2)

        @pl.when(chunk == 0)
        def _():
            enter(2)

        @pl.when(chunk < 2)
        def _():
            send_y(chunk + 1, 0)
            send_y(chunk + 1, 1)

        @pl.loop(0, 3)
        def _(i):
            m, slot = group(i), chunk + 3
            arrive(slot, m, i, lambda: None)

            @pl.when(chunk < 2)
            def _():
                send(chunk + 1, m, 0, 4)

            rim_product(slot, m)

            def write(x, here, mid, total):
                fil[chunk, x, :, here] = 2.0 * total - cen[chunk, x, :, mid]

            stencil(slot, m, write)
            band_copy(chunk, m, 1 - band).start()

            @pl.when(chunk == 2)
            def _():
                own_products(m)

        fil_out(chunk).start()

    def cross_products(m):
        for chunk in range(3):
            band_copy(chunk, m, band).wait_recv()
        mine, theirs = rows(fil, m, 6 * band, 6), rows(oth, m, 6 * band, 6)
        first, second = jnp.where(band == 0, mine, theirs), jnp.where(band == 0, theirs, mine)
        acc[:, 64:88] += folded(second, first)

    @pl.loop(0, 3)
    def _(i):
        @pl.when(i == 2)
        def _():
            for m in range(3):
                band_copy(2, m, 1 - band).wait_send()

            @pl.when(band == 0)
            def _():
                for m in range(3):
                    band_copy(2, m, 0).start()

        cross_products(group(i))

    v = acc[...]
    alone = jnp.where(lax.broadcasted_iota(jnp.int32, (24, 128), 1) < 24, v, 0.0)
    cross = v - alone
    tail = pltpu.roll(alone[16:], 72, 1)
    part[0] = (
        jnp.where(band == 0, alone[:16], pltpu.roll(alone[:16], 24, 1))
        + pltpu.roll(cross[:16], 112, 1)
        + jnp.concatenate([jnp.where(band == 0, tail, 0.0) + pltpu.roll(cross[16:], 32, 1), jnp.where(band == 0, 0.0, tail)], 0)
    )

    def settle_early():
        @pl.when(band == 1)
        def _():
            last_out(1).start()

            @pl.loop(0, 2)
            def _(chunk):
                for m in range(3):
                    band_copy(chunk, m, 0).wait_recv()
                oth_out(chunk).start()

        @pl.loop(0, 6)
        def _(slot):
            for m in range(3):
                for copy in copies(slot, m):
                    copy.wait_send()
            for face in range(2):

                def wait_outer():
                    for copy in y_copies(slot, face, odds[0]):
                        copy.wait_send()

                for copy in y_copies(slot, face, 1 - odds[0]):
                    copy.wait_send()
                for_outer(face, wait_outer)
            for copy in forward_copies(slot, 0):
                copy.wait_send()

    def settle_late():
        @pl.loop(0, 2)
        def _(chunk):
            for m in range(3):
                band_copy(chunk, m, 1 - band).wait_send()

            @pl.when(band == 0)
            def _():
                for m in range(3):
                    band_copy(chunk, m, 0).wait_send()

            @pl.when(band == 1)
            def _():
                oth_out(chunk).wait()

        for chunk in range(3):
            fil_out(chunk).wait()

        @pl.when(band == 0)
        def _():
            for m in range(3):
                band_copy(2, m, 0).wait_send()

        @pl.when(band == 1)
        def _():
            for m in range(3):
                band_copy(2, m, 0).wait_recv()
            last_out(0).start()
            last_out(1).wait()

    index = 0
    for number, stage in enumerate(stages):
        moves = []
        for partner in stage:
            moves.append(
                pltpu.make_async_remote_copy(
                    part.at[number], got.at[index], sum_send.at[index], sum_recv.at[index],
                    device_id=partner, device_id_type=MESH,
                )
            )
            index += 1
        for move in moves:
            move.start()
        (settle_early, lambda: None, settle_late)[number]()
        for move in moves:
            move.wait_recv()
        terms = [part[number]] + [got[index - len(stage) + k] for k in range(len(stage))]
        while len(terms) > 1:
            terms = [a + b for a, b in zip(terms[::2], terms[1::2])]
        if number < 2:
            part[number + 1] = terms[0]
        else:
            gram[...] = terms[0]
        for move in moves:
            move.wait_send()

    @pl.when(band == 1)
    def _():
        last_out(0).wait()


def filter_call(lines, pot):
    wh, wl = yz_weights()
    sel = face_weights()
    any_space = pl.BlockSpec(memory_space=pl.ANY)
    chunk = (3, CX, 8, CYZ)
    vm = pltpu.VMEM
    return pl.pallas_call(
        filter_kernel,
        out_shape=(
            jax.ShapeDtypeStruct(chunk, F32),
            jax.ShapeDtypeStruct(chunk, F32),
            jax.ShapeDtypeStruct((16, 128), F32),
        ),
        in_specs=[any_space] * 5,
        out_specs=(any_space, any_space, pl.BlockSpec(memory_space=pltpu.VMEM)),
        scratch_shapes=[
            vm((24 * 216, 128), F32),
            vm((216, 128), F32),
            vm(wh.shape, BF),
            vm(wl.shape, BF),
            vm(sel.shape, BF),
            vm((6, CX, 8, LANES), F32),
            vm((6, 2, 6, 8, CYZ), F32),
            vm((6, 9, 8, 384), F32),
            vm((6, 9, 8, 384), F32),
            vm((6, 9, 8, 384), F32),
            vm((6, 9, 8, 384), F32),
            vm((6, 2, 2, 8, 128), F32),
            vm((6, 2, 2, 8, 128), F32),
            vm((6, 2, 2, 8, 128), F32),
            vm((6, 2, 2, 8, 128), F32),
            vm((6, 2, 8, 128), F32),
            vm((6, 96, LANES), BF),
            vm((6, 96, LANES), BF),
            vm((96, 768), F32),
            vm(chunk, F32),
            vm(chunk, F32),
            vm((24, 128), F32),
            vm((3, 16, 128), F32),
            vm((13, 16, 128), F32),
            pltpu.SemaphoreType.DMA((7,)),
            pltpu.SemaphoreType.DMA((7,)),
            pltpu.SemaphoreType.DMA((6, 3, 6)),
            pltpu.SemaphoreType.DMA((6, 3, 6)),
            pltpu.SemaphoreType.DMA((6, 2, 2, 2)),
            pltpu.SemaphoreType.DMA((6, 2, 2, 2)),
            pltpu.SemaphoreType.DMA((6, 2)),
            pltpu.SemaphoreType.DMA((3, 3, 2)),
            pltpu.SemaphoreType.DMA((3, 3, 2)),
            pltpu.SemaphoreType.DMA((13,)),
            pltpu.SemaphoreType.DMA((13,)),
        ],
        compiler_params=pltpu.CompilerParams(collective_id=0, has_side_effects=True, vmem_limit_bytes=56 << 20),
        name="filter",
    )(lines, pot, jnp.asarray(wh), jnp.asarray(wl), jnp.asarray(sel))


def rotate_kernel(low, high, gram, out, mine, theirs, inverse, lines, sems, out_sems):
    band = lax.axis_index("band")

    def loads(x):
        own_load = pltpu.make_async_copy(low.at[:, x], mine.at[:, x], sems.at[0, x])
        return own_load, pltpu.make_async_copy(high.at[:, x], theirs.at[:, x], sems.at[1, x])

    for x in range(CX):
        loads(x)[0].start()

        @pl.when(band == 1)
        def _():
            loads(x)[1].start()

    g = gram[...] * (1.0 / (64 * CX * CYZ))
    blank = jnp.zeros((24, 16), F32)
    row, col = (lax.broadcasted_iota(jnp.int32, (48, 64), d) for d in range(2))
    unit = (row == col).astype(F32)
    first = jnp.concatenate([g[:, 0:24], g[0:8, 72:96]], 0)
    second = jnp.concatenate([g[:, 24:48], g[8:16, 72:96]], 0)
    cross = jnp.concatenate([g[:, 48:72], g[0:8, 96:120]], 0)
    turned = lax.dot_general(unit[:24, :24], cross, (((1,), (1,)), ((), ())), precision=lax.Precision.HIGHEST)
    left = jnp.concatenate(
        [jnp.concatenate([first, turned, blank], 1), jnp.concatenate([cross, second, blank], 1)], 0
    )
    table = jnp.concatenate([left, unit], 1)
    rows = lax.broadcasted_iota(jnp.int32, (48, 128), 0)
    for k in range(0, 48, 2):
        one = jnp.broadcast_to(table[:, k : k + 1], (48, 128))
        two = jnp.broadcast_to(table[:, k + 1 : k + 2], (48, 128))
        a, b, c = one[k : k + 1], one[k + 1 : k + 2], two[k + 1 : k + 2]
        upper, lower = table[k : k + 1], table[k + 1 : k + 2]
        inverse[k : k + 1, :] = upper * lax.rsqrt(a)
        ratio = b / a
        inverse[k + 1 : k + 2, :] = (lower - ratio * upper) * lax.rsqrt(c - ratio * b)
        if k < 46:
            scale = 1.0 / (a * c - b * b)
            below = rows > k + 1
            table = (
                table
                - jnp.where(below, one, 0.0) * ((c * upper - b * lower) * scale)
                - jnp.where(below, two, 0.0) * ((a * lower - b * upper) * scale)
            )

    def sent(quarter):
        at = pl.ds(72 * quarter, 72)
        return pltpu.make_async_copy(lines.reshape(24, 216, 128).at[:, at], out.at[:, at], out_sems.at[quarter])

    def rotate(matrix, sources):
        mh, ml = split(matrix)
        left = jnp.concatenate([jnp.concatenate([mh, mh], 1), jnp.concatenate([ml, jnp.zeros_like(ml)], 1)], 0)
        for x in range(CX):
            for ready in range(x, x + 4) if x % 4 == 0 else ():
                for load in loads(ready)[: len(sources)]:
                    load.wait()
            v = [source[:, x].reshape(24, CYZ) for source in sources]
            vh, vl = split(jnp.concatenate(v, 0) if len(v) > 1 else v[0])
            made = dot(left, jnp.concatenate([vh, vl], 0))
            made = made[:24] + made[24:]
            for t in range(18):
                lines[pl.ds(18 * x + t, 24, stride=216), :] = made[:, 128 * t : 128 * t + 128]
            if x % 4 == 3:
                sent(x // 4).start()

    @pl.when(band == 0)
    def _():
        rotate(inverse[0:24, 64:88], [mine])

    @pl.when(band == 1)
    def _():
        rotate(jnp.concatenate([inverse[24:48, 88:112], inverse[24:48, 64:88]], 1), [mine, theirs])

    for quarter in range(3):
        sent(quarter).wait()


def rotate_call(mine, theirs, gram):
    any_space = pl.BlockSpec(memory_space=pl.ANY)
    vm = pltpu.VMEM
    return pl.pallas_call(
        rotate_kernel,
        out_shape=jax.ShapeDtypeStruct((24, 216, 128), F32),
        in_specs=[any_space, any_space, pl.BlockSpec(memory_space=pltpu.VMEM)],
        out_specs=any_space,
        scratch_shapes=[
            vm((3, CX, 8, CYZ), F32),
            vm((3, CX, 8, CYZ), F32),
            vm((48, 128), F32),
            vm((24 * 216, 128), F32),
            pltpu.SemaphoreType.DMA((2, CX)),
            pltpu.SemaphoreType.DMA((3,)),
        ],
        compiler_params=pltpu.CompilerParams(vmem_limit_bytes=56 << 20),
        name="rotate",
    )(mine, theirs, gram)


def body(orbitals, potential):
    mine, theirs, gram = filter_call(orbitals.reshape(24 * 216, 128), potential.reshape(216, 128))
    return rotate_call(mine, theirs, gram).reshape(orbitals.shape)


def solution(mesh):
    return jax.shard_map(
        body,
        mesh=mesh,
        in_specs=(P("band", "dom", None, None), P("dom", None, None)),
        out_specs=P("band", "dom", None, None),
        check_vma=False,
    )
```
